128 devices in a mesh: role: 2 (over x_lo), seq: 8 (over z, core), tp: 8 (over y, x_hi).
Axes of the slice: x: 4 (x_hi: 2, x_lo: 2; x = x_hi * 2 + x_lo), y: 4, z: 4, core: 2. Of those that a mesh axis runs over, the one named last changes fastest.
Arguments:
- hidden: bfloat16 [4096, 8192], P(('role', 'seq')), may hold values from -11 to 11
- w_query: bfloat16 [8192, 4096], P(None, 'tp'), may hold values from -0.0625 to 0.0625
- w_key: bfloat16 [896, 4096], P(None, 'tp'), may hold values from -0.1875 to 0.1875
- w_value: bfloat16 [896, 4096], P(None, 'tp'), may hold values from -0.1875 to 0.1875
- enc_gain: float32 [896], replicated, may hold values from 0.1 to 1.9
- w_in: bfloat16 [896, 1792], replicated, may hold values from -0.1875 to 0.1875
- w_out: bfloat16 [1792, 896], replicated, may hold values from -0.125 to 0.125
- db_states: bfloat16 [256, 128, 896], P(('role', 'seq'), 'tp'), may hold values from -24 to 24
- neighbours: int32 [64, 2], P(('role', 'seq')), may hold values from 0 to 255, as said below
- d_attended: bfloat16 [4096, 4096], P(('role', 'seq'), 'tp'), may hold values from -24 to 24
Outputs:
- attended: bfloat16 [4096, 4096], P(('role', 'seq'), 'tp')
- grad_rows: bfloat16 [256, 128, 896], P(('role', 'seq'), 'tp')
The draws below stay inside these ranges and needn't reach their ends.
Inputs may be any that keep to these rules, and one draw needn't show every extreme that they name: Database rows; shard g of role+seq holds rows g * 16 to (g + 1) * 16 - 1. Of the 8 neighbours of the stretches on one index of role+seq, at most 2 lie in one shard (repeats counted), and exactly 2 in some shard.
All inputs are finite; a program needn't handle non-finite values.
Results may differ from the reference program's by a relative error of at most 0.02.
The reference program's roundings to bfloat16 on the way count: a program that leaves them out, or rounds other values in their place, can miss the bound.
Values may be sent and summed in bfloat16 or wider, within the bound.
A program may use at most 128 MiB of HBM per device.

```python
import math
import jax
import jax.numpy as jnp
from jax import lax

D = 8192
HEADS = 32
HD = 128
DE = 896
FE = 1792
NT = 128
STRETCH = 64
K_NB = 2
TOK_DEV = 256
R_DEV = 16
GROUPS = 16
TOKENS = 4096
CH_DEV = 4
STRETCHES = 64
DB_ROWS = 256
FEAT = 4096
N_ROLE = 2
N_SEQ = 8


def draw_hidden(key, part):
    key = jax.random.fold_in(key, 5)
    base_key = jax.random.fold_in(key, 0)
    base = jax.random.truncated_normal(base_key, -6.0, 6.0, (TOKENS, D), jnp.float32)
    return base.astype(jnp.bfloat16)


def draw_db_states(key, part):
    key = jax.random.fold_in(key, 7)
    base_key, column_key, token_key = jax.random.split(key, 3)
    columns = jnp.exp(jax.random.uniform(column_key, (1, 1, DE), jnp.float32, math.log(0.3), math.log(3.0)))
    tokens = jnp.exp(jax.random.uniform(token_key, (DB_ROWS, NT, 1), jnp.float32, math.log(0.5), math.log(2.0)))
    base = jax.random.truncated_normal(base_key, -4.0, 4.0, (DB_ROWS, NT, DE), jnp.float32)
    return (base * columns * tokens).astype(jnp.bfloat16)


def draw_neighbours(key, part):
    key = jax.random.fold_in(key, 11)
    hot_key, shuffle_key, order_key, row_key = jax.random.split(key, 4)
    groups = DB_ROWS // R_DEV
    slot_count = CH_DEV * K_NB
    hot_owner = jax.random.randint(hot_key, (), 0, groups)
    shuffles = jax.vmap(lambda sub_key: jax.random.permutation(sub_key, groups - 1))(jax.random.split(shuffle_key, groups))
    unit_of = jnp.maximum(jnp.arange(slot_count) - 2, 0) // 2 % (groups - 1)
    others = shuffles[:, unit_of]
    others = others + (others >= hot_owner).astype(jnp.int32)
    owners = jnp.where(jnp.arange(slot_count)[None, :] < 2, hot_owner, others)
    orders = jax.vmap(lambda sub_key: jax.random.permutation(sub_key, slot_count))(jax.random.split(order_key, groups))
    owners = jnp.take_along_axis(owners, orders, axis=1)
    row_pick = jax.random.randint(row_key, (groups, slot_count), 0, R_DEV)
    return (owners * R_DEV + row_pick).reshape(STRETCHES, K_NB).astype(jnp.int32)


def shard_levels(stream_key, shape, cuts, low, high):
    level, own = 1.0, jax.random.fold_in(stream_key, 6)
    for position, parts in cuts:
        draws = jnp.exp(jax.random.uniform(jax.random.fold_in(own, position), (parts,), jnp.float32, low / len(cuts), high / len(cuts)))
        level = level * jnp.repeat(draws, shape[position] // parts).reshape([-1 if axis == position else 1 for axis in range(len(shape))])
    return level


def scatter_about(own_key, dims, width, reach, pieces=(), kind=jnp.bfloat16):
    values = width * jax.random.normal(own_key, dims, jnp.float32)
    if pieces:
        values = values * shard_levels(own_key, dims, pieces, -0.22, 0.18)
    return jnp.clip(values, -reach, reach).astype(kind)


def setup_inputs(seed: int = 0) -> dict:
    arg_keys = jax.random.split(jax.random.key(seed), 11)
    return {
        "hidden": draw_hidden(jax.random.fold_in(arg_keys[10], 71), 0),
        "w_query": scatter_about(arg_keys[1], (D, FEAT), D ** -0.5, 0.0625, ((1, 8),)),
        "w_key": scatter_about(arg_keys[2], (DE, FEAT), DE ** -0.5, 0.1875, ((1, 8),)),
        "w_value": scatter_about(arg_keys[3], (DE, FEAT), DE ** -0.5, 0.1875, ((1, 8),)),
        "enc_gain": jnp.clip(1.0 + 0.18 * jax.random.normal(arg_keys[4], (DE,), jnp.float32), 0.1, 1.9),
        "w_in": scatter_about(arg_keys[5], (DE, FE), DE ** -0.5, 0.1875),
        "w_out": scatter_about(arg_keys[6], (FE, DE), FE ** -0.5, 0.125),
        "db_states": draw_db_states(jax.random.fold_in(arg_keys[10], 71), 0),
        "neighbours": draw_neighbours(jax.random.fold_in(arg_keys[10], 71), 0),
        "d_attended": scatter_about(arg_keys[9], (TOKENS, FEAT), 4.0, 24.0, ((0, 16), (1, 8))),
    }


EPS = 1e-06

def encode(flat_rows, enc_gain, w_in, w_out):
    row_values = flat_rows.astype(jnp.float32)
    inverse = lax.rsqrt(lax.optimization_barrier(jnp.mean(row_values * row_values, axis=-1, keepdims=True)) + EPS)
    normed = (row_values * inverse * enc_gain).astype(jnp.bfloat16)
    pre_act = jnp.dot(normed, w_in, preferred_element_type=jnp.float32)
    active = jax.nn.gelu(pre_act).astype(jnp.bfloat16)
    encoded = (row_values + jnp.dot(active, w_out, preferred_element_type=jnp.float32)).astype(jnp.bfloat16)
    return (encoded, inverse, pre_act)

def encode_back(flat_rows, inverse, pre_act, row_grad, enc_gain, w_in, w_out):
    row_values = flat_rows.astype(jnp.float32)
    upstream = row_grad.astype(jnp.bfloat16)
    d_act = jnp.dot(upstream, w_out.T, preferred_element_type=jnp.float32)
    d_pre = jax.vjp(jax.nn.gelu, pre_act)[1](d_act)[0]
    d_norm = jnp.dot(d_pre.astype(jnp.bfloat16), w_in.T, preferred_element_type=jnp.float32)
    scaled = d_norm * enc_gain
    cubed = inverse * inverse * inverse
    back_term = inverse * scaled - row_values * cubed * lax.optimization_barrier(jnp.mean(scaled * row_values, axis=-1, keepdims=True))
    return (row_grad + back_term).astype(jnp.bfloat16)

def attend(queries, key_rows, value_rows, score_scale):
    scores = jnp.einsum('bqhe,bkhe->bhqk', queries.astype(jnp.float32), key_rows.astype(jnp.float32)) * score_scale
    maximum = lax.optimization_barrier(jnp.max(scores, axis=-1, keepdims=True))
    weights = jnp.exp(scores - maximum)
    probability = weights / lax.optimization_barrier(jnp.sum(weights, axis=-1, keepdims=True))
    rounded = probability.astype(jnp.bfloat16)
    outputs = jnp.einsum('bhqk,bkhe->bqhe', rounded.astype(jnp.float32), value_rows.astype(jnp.float32))
    return (outputs, probability, rounded)

def attend_back(queries, value_rows, probability, rounded, cotangent, score_scale):
    value_grads = jnp.einsum('bhqk,bqhe->bkhe', rounded.astype(jnp.float32), cotangent.astype(jnp.float32))
    dprobs = jnp.einsum('bqhe,bkhe->bhqk', cotangent.astype(jnp.float32), value_rows.astype(jnp.float32))
    centre = lax.optimization_barrier(jnp.sum(probability * dprobs, axis=-1, keepdims=True))
    dscores = (probability * (dprobs - centre)).astype(jnp.bfloat16)
    key_grads = jnp.einsum('bhqk,bqhe->bkhe', dscores.astype(jnp.float32), queries.astype(jnp.float32)) * score_scale
    return (key_grads, value_grads)

def reference(hidden, w_query, w_key, w_value, enc_gain, w_in, w_out, db_states, neighbours, d_attended):
    score_scale = HD ** (-0.5)
    seq_len = TOK_DEV * N_SEQ
    stretch_seq = seq_len // STRETCH
    span = K_NB * NT
    flat_ids = neighbours.reshape(-1).astype(jnp.int32)
    cited = jnp.take(db_states, flat_ids, axis=0).reshape(-1, DE)
    encoded, inverse, pre_act = encode(cited, enc_gain, w_in, w_out)
    key_rows = jnp.dot(encoded, w_key, preferred_element_type=jnp.float32).astype(jnp.bfloat16)
    value_rows = jnp.dot(encoded, w_value, preferred_element_type=jnp.float32).astype(jnp.bfloat16)
    zero_stretch = ((0, 0), (1, 0), (0, 0), (0, 0), (0, 0))
    key_rows = jnp.pad(key_rows.reshape(N_ROLE, stretch_seq, span, HEADS, HD), zero_stretch)
    key_rows = key_rows.reshape(N_ROLE * (stretch_seq + 1), span, HEADS, HD)
    value_rows = jnp.pad(value_rows.reshape(N_ROLE, stretch_seq, span, HEADS, HD), zero_stretch)
    value_rows = value_rows.reshape(N_ROLE * (stretch_seq + 1), span, HEADS, HD)
    queries = jnp.dot(hidden, w_query, preferred_element_type=jnp.float32).astype(jnp.bfloat16)
    edges = ((0, 0), (1, STRETCH - 1), (0, 0), (0, 0))
    block_q = jnp.pad(queries.reshape(N_ROLE, seq_len, HEADS, HD), edges)
    block_q = block_q.reshape(N_ROLE * (stretch_seq + 1), STRETCH, HEADS, HD)
    outputs, probability, rounded = attend(block_q, key_rows, value_rows, score_scale)
    outputs = outputs.reshape(N_ROLE, (stretch_seq + 1) * STRETCH, HEADS * HD)[:, 1:seq_len + 1]
    attended = outputs.reshape(TOKENS, HEADS * HD).astype(jnp.bfloat16)
    block_d = jnp.pad(d_attended.reshape(N_ROLE, seq_len, HEADS, HD), edges)
    block_d = block_d.reshape(N_ROLE * (stretch_seq + 1), STRETCH, HEADS, HD)
    key_grads, value_grads = attend_back(block_q, value_rows, probability, rounded, block_d, score_scale)
    key_back = key_grads.reshape(N_ROLE, stretch_seq + 1, span, HEADS * HD)[:, 1:]
    key_back = key_back.reshape(-1, HEADS * HD).astype(jnp.bfloat16)
    value_back = value_grads.reshape(N_ROLE, stretch_seq + 1, span, HEADS * HD)[:, 1:]
    value_back = value_back.reshape(-1, HEADS * HD).astype(jnp.bfloat16)
    slot_grad = jnp.dot(key_back, w_key.T, preferred_element_type=jnp.float32)
    slot_grad = slot_grad + jnp.dot(value_back, w_value.T, preferred_element_type=jnp.float32)
    row_grad = jax.ops.segment_sum(slot_grad.reshape(STRETCHES * K_NB, NT * DE), flat_ids, num_segments=DB_ROWS)

    def backward_group(pair):
        rows_block, grad_block = pair
        unused, inverse_block, pre_block = encode(rows_block, enc_gain, w_in, w_out)
        return encode_back(rows_block, inverse_block, pre_block, grad_block, enc_gain, w_in, w_out)
    grads = lax.map(backward_group, (db_states.reshape(GROUPS, R_DEV * NT, DE), row_grad.reshape(GROUPS, R_DEV * NT, DE)))
    return (attended, grads.reshape(DB_ROWS, NT, DE))
```

```python
import jax
import jax.numpy as jnp
from jax import lax
from jax.experimental import pallas as pl
from jax.experimental.pallas import tpu as pltpu
from jax.sharding import PartitionSpec as P

HD = 128
STRETCH = 64
EPS = 1e-06
MESH = pl.DeviceIdType.MESH
BF16 = jnp.bfloat16
F32 = jnp.float32
GELU_A = 0.7978845608028654
GELU_B = 0.044715

GROUPS = 16
SEQ = 8
ROWS = 16
SLOTS = 8
PIECE = 16
WIDTH = 896
FFN = 1792
TOK = 256
DM = 8192
FEAT = 512
BLOCK = SLOTS * PIECE
HALF = BLOCK // 2
CHUNKS = ((0, 512), (512, 384))
QK = 1024
QSTEPS = DM // QK


def dot(a, b):
    return jnp.dot(a, b, preferred_element_type=F32)


def dot_nt(a, b):
    return lax.dot_general(a, b, (((1,), (1,)), ((), ())), preferred_element_type=F32)


def dot_tn(a, b):
    return lax.dot_general(a, b, (((0,), (0,)), ((), ())), preferred_element_type=F32)


def kernel(
    nb, db_hbm, hid_hbm, wq_hbm, wk_hbm, wv_hbm, gain, win_hbm, wout_hbm, cot_hbm,
    att_out, grad_out,
    ids, row_tab, own_tab, slot_tab,
    db, win, wout, w2, hid, wq, cot,
    normed, active, gd, inv_s, onehot, qacc, qs, cs, qn, cn, obuf, on,
    enc0, enc1, sa0, sa1, ra0, ra1, g0, g1, kvacc, kv, kgv,
    ca0, ca1, cb0, cb1, cx0, cx1, ta0, ta1, tb0, tb1, tx0, tx1,
    fin0, fin1, sd0, sd1, rd0, rd1, rgrad, dnorm,
    lsem, ids_ss, ids_rs, a_ss, a_rs, d_ss, d_rs, b_ss, b_rs, c_ss, c_rs, q_ss, q_rs,
):
    enc, sa, ra, g = (enc0, enc1), (sa0, sa1), (ra0, ra1), (g0, g1)
    ca, cb, cx = (ca0, ca1), (cb0, cb1), (cx0, cx1)
    ta, tb, tx = (ta0, ta1), (tb0, tb1), (tx0, tx1)
    fin, sd, rd = (fin0, fin1), (sd0, sd1), (rd0, rd1)
    r = lax.axis_index("role")
    s = lax.axis_index("seq")
    t = lax.axis_index("tp")
    y = t // 2
    xh = t % 2
    me = r * SEQ + s
    x = xh * 2 + r
    t_plus = y * 2 + ((x + 1) % 4) // 2
    t_minus = y * 2 + ((x + 3) % 4) // 2
    other = 1 - r
    up = (y + 1) % 4
    down = (y + 3) % 4
    far = (y + 2) % 4
    dev_up = (r, s, up * 2 + xh)
    dev_down = (r, s, down * 2 + xh)
    dev_x = (r, s, y * 2 + 1 - xh)
    dev_next = (r, (s + 1) % SEQ, t)
    dev_prev = (r, (s + SEQ - 1) % SEQ, t)

    def remote(src, dst, ss, rs, dev):
        return pltpu.make_async_remote_copy(
            src_ref=src, dst_ref=dst, send_sem=ss, recv_sem=rs, device_id=dev, device_id_type=MESH
        )

    barrier = pltpu.get_barrier_semaphore()

    def greet(dev):
        pl.semaphore_signal(barrier, inc=1, device_id=dev, device_id_type=MESH)

    def greet_same(j, c):
        greet((r, (s + j) % SEQ, t))
        return c

    def greet_cross(j, c):
        greet((other, (s + j) % SEQ, t_plus))
        greet((other, (s + j) % SEQ, t_minus))
        return c

    lax.fori_loop(1, SEQ, greet_same, 0)
    lax.fori_loop(0, SEQ, greet_cross, 0)
    greet(dev_up)
    greet(dev_down)
    greet(dev_x)

    loads = []

    def load(src, dst):
        cp = pltpu.make_async_copy(src, dst, lsem.at[len(loads)])
        cp.start()
        loads.append(cp)
        return cp

    l_db = load(db_hbm, db)
    l_win = load(win_hbm, win)
    l_wout = load(wout_hbm, wout)
    l_cot = load(cot_hbm, cot)
    l_hid = load(hid_hbm, hid)
    l_wq = [
        load(wq_hbm.at[pl.ds(i * QK, QK)], wq.at[pl.ds(i * QK, QK)]) for i in range(QSTEPS)
    ]
    l_wk = load(wk_hbm, w2.at[:, pl.ds(0, FEAT)])
    l_wv = load(wv_hbm, w2.at[:, pl.ds(FEAT, FEAT)])

    def copy_ids(i, c):
        ids[me, i] = nb[i // 2, i % 2]
        return c

    lax.fori_loop(0, SLOTS, copy_ids, 0)

    pl.semaphore_wait(barrier, 26)

    def ids_same(j):
        dev = (r, (s + j) % SEQ, t)
        return remote(ids.at[me], ids.at[me], ids_ss.at[j], ids_rs.at[j], dev)

    def ids_cross(j):
        dev = (other, (s + j) % SEQ, t_plus)
        return remote(ids.at[me], ids.at[me], ids_ss.at[SEQ + j], ids_rs.at[SEQ + j], dev)

    def each_same(make, act):
        def step(j, c):
            act(make(j))
            return c

        lax.fori_loop(1, SEQ, step, 0)

    def each_cross(make, act):
        def step(j, c):
            act(make(j))
            return c

        lax.fori_loop(0, SEQ, step, 0)

    start = lambda cp: cp.start()
    wait_recv = lambda cp: cp.wait_recv()
    wait_send = lambda cp: cp.wait_send()

    each_same(ids_same, start)
    each_cross(ids_cross, start)

    l_db.wait()
    xv = db[...].reshape(TOK, WIDTH).astype(F32)
    inverse = lax.rsqrt(jnp.mean(xv * xv, axis=-1, keepdims=True) + EPS)
    inv_s[...] = jnp.broadcast_to(inverse, (TOK, 128))
    normed[...] = (xv * inverse * gain[...]).astype(BF16)
    l_win.wait()

    def first_layer(c, carry):
        cols = pl.ds(pl.multiple_of(c * 256, 256), 256)
        pre = dot(normed[...], win[:, cols])
        sq = pre * pre
        th = jnp.tanh(GELU_A * (pre + GELU_B * (sq * pre)))
        cdf = 0.5 * (1.0 + th)
        active[:, cols] = (pre * cdf).astype(BF16)
        gd[:, cols] = cdf + pre * (0.5 * GELU_A) * (1.0 - th * th) * (1.0 + 3.0 * GELU_B * sq)
        return carry

    lax.fori_loop(0, FFN // 256, first_layer, 0)
    l_wout.wait()

    def encode(c):
        lo, n = CHUNKS[c]
        rows = db[:, :, lo:lo + n].reshape(TOK, n).astype(F32)
        out = rows + dot(active[...], wout[:, lo:lo + n])
        enc[c][...] = out.astype(BF16).reshape(ROWS, PIECE, n)

    encode(0)

    each_same(ids_same, wait_recv)
    each_cross(ids_cross, wait_recv)

    def row_step(q, c):
        cnt = jnp.int32(0)
        row0 = jnp.int32(0)
        row1 = jnp.int32(0)
        for k in range(SLOTS):
            v = ids[q, k] - me * ROWS
            hit = (v >= 0) & (v < ROWS)
            row0 = jnp.where(hit & (cnt == 0), v, row0)
            row1 = jnp.where(hit & (cnt == 1), v, row1)
            cnt = cnt + hit.astype(jnp.int32)
        row_tab[0, q] = row0
        row_tab[1, q] = row1
        row_tab[2, q] = cnt
        return c

    lax.fori_loop(0, GROUPS, row_step, 0)

    def fill(c):
        def step(q, carry):
            sa[c][2 * q] = enc[c][row_tab[0, q]]
            sa[c][2 * q + 1] = enc[c][row_tab[1, q]]
            return carry

        lax.fori_loop(0, GROUPS, step, 0)
        ra[c][pl.ds(2 * me, 2)] = sa[c][pl.ds(2 * me, 2)]

    def out_same(src, dst, ss, rs, c):
        def make(j):
            sj = (s + j) % SEQ
            q = r * SEQ + sj
            return remote(
                src[c].at[pl.ds(2 * q, 2)], dst[c].at[pl.ds(2 * me, 2)],
                ss.at[c, j], rs.at[c, j], (r, sj, t),
            )

        return make

    def out_cross(src, dst, ss, rs, c, level, tdev):
        def make(j):
            sj = (s + j) % SEQ
            q = other * SEQ + sj
            at = SEQ * (1 + level) + j
            return remote(
                src[c].at[2 * q + level], dst[c].at[2 * me + level],
                ss.at[c, at], rs.at[c, at], (other, sj, tdev),
            )

        return make

    def exchange(src, dst, ss, rs, c, t0, t1, act):
        each_same(out_same(src, dst, ss, rs, c), act)
        each_cross(out_cross(src, dst, ss, rs, c, 0, t0), act)
        each_cross(out_cross(src, dst, ss, rs, c, 1, t1), act)

    def a_do(c, act):
        exchange(sa, ra, a_ss, a_rs, c, t_plus, t_minus, act)

    fill(0)
    a_do(0, start)
    encode(1)
    fill(1)
    a_do(1, start)

    def own_step(k, c):
        v = ids[me, k]
        owner = v // ROWS
        rank = jnp.int32(0)
        for e in range(SLOTS):
            same = (ids[me, e] // ROWS == owner) & (e < k)
            rank = rank + same.astype(jnp.int32)
        own_tab[0, k] = owner * 2 + rank
        return c

    lax.fori_loop(0, SLOTS, own_step, 0)

    def slot_step(q, c):
        slot = jnp.int32(0)
        for k in range(SLOTS):
            slot = jnp.where(own_tab[0, k] == q, k, slot)
        slot_tab[0, q] = slot
        return c

    lax.fori_loop(0, 2 * GROUPS, slot_step, 0)

    lane_k = lax.broadcasted_iota(jnp.int32, (8, 512), 1) // PIECE

    def col_step(q, cols):
        cnt = row_tab[2, q]
        first = jnp.where(cnt > 0, row_tab[0, q], -1)
        second = jnp.where(cnt > 1, row_tab[1, q], -1)
        cols = jnp.where(lane_k == 2 * q, first, cols)
        return jnp.where(lane_k == 2 * q + 1, second, cols)

    cols = lax.fori_loop(0, GROUPS, col_step, jnp.full((8, 512), -1, jnp.int32))
    row_i = lax.broadcasted_iota(jnp.int32, (TOK, 512), 0)
    col_i = lax.broadcasted_iota(jnp.int32, (TOK, 512), 1)
    match = (row_i // PIECE == cols[0:1, :]) & (row_i % PIECE == col_i % PIECE)
    onehot[...] = jnp.where(match, 1.0, 0.0).astype(BF16)

    def shift(k, buf, landing):
        return remote(buf.at[pl.ds(192, 64)], landing, q_ss.at[k], q_rs.at[k], dev_prev)

    l_cot.wait()
    cs[...] = pltpu.roll(cot[...].astype(F32), TOK - (STRETCH - 1), 0).astype(BF16)
    shift(0, cs, cn).start()
    l_hid.wait()
    for i in range(QSTEPS):
        l_wq[i].wait()
        part = dot(hid[:, i * QK:(i + 1) * QK], wq[pl.ds(i * QK, QK), :])
        if i == 0:
            qacc[...] = part
        else:
            qacc[...] += part
    qs[...] = pltpu.roll(qacc[...].astype(BF16).astype(F32), TOK - (STRETCH - 1), 0).astype(BF16)
    shift(1, qs, qn).start()

    bo = t
    bp = y * 2 + 1 - xh

    def b_copy(c, k):
        ss, rs = b_ss.at[c, k], b_rs.at[c, k]
        if k == 0:
            return remote(g[c].at[bo], g[c].at[bo], ss, rs, dev_x)
        if k in (1, 2):
            return remote(g[c].at[bo], g[c].at[bo], ss, rs, dev_up if k == 1 else dev_down)
        if k in (3, 4):
            return remote(g[c].at[bp], g[c].at[bp], ss, rs, dev_up if k == 3 else dev_down)
        h = xh if k in (5, 6) else 1 - xh
        if k in (5, 7):
            part = g[c].at[down * 2 + h, pl.ds(0, HALF)]
            return remote(part, part, ss, rs, dev_up)
        part = g[c].at[up * 2 + h, pl.ds(HALF, HALF)]
        return remote(part, part, ss, rs, dev_down)

    def select(c):
        def step(k, carry):
            n = CHUNKS[c][1]
            g[c][bo, pl.ds(pl.multiple_of(k * PIECE, PIECE), PIECE)] = ra[c][own_tab[0, k]]
            return carry

        lax.fori_loop(0, SLOTS, step, 0)

    def project(c, b):
        lo, n = CHUNKS[c]
        part = dot(g[c][b], w2[lo:lo + n, :])
        if c == 0:
            kvacc[b] = part
        else:
            out = (kvacc[b] + part).astype(BF16)
            for u in range(4):
                kv[u, pl.ds(pl.multiple_of(b * 32, 32), 32), :] = out[u * 32:(u + 1) * 32]

    def begin(c):
        a_do(c, wait_recv)
        select(c)
        for k in range(3):
            b_copy(c, k).start()

    def b_wait(c, *ks):
        for k in ks:
            b_copy(c, k).wait_recv()

    def b_start(c, *ks):
        for k in ks:
            b_copy(c, k).start()

    begin(0)
    l_wk.wait()
    l_wv.wait()
    project(0, bo)
    b_wait(0, 0)
    b_start(0, 3, 4)
    project(0, bp)
    b_wait(0, 1)
    b_start(0, 5)
    b_wait(0, 2)
    b_start(0, 6)
    begin(1)
    project(0, down * 2 + xh)
    project(0, up * 2 + xh)
    b_wait(0, 3)
    b_start(0, 7)
    b_wait(0, 4)
    b_start(0, 8)
    b_wait(1, 0)
    b_start(1, 3, 4)
    project(0, down * 2 + 1 - xh)
    project(0, up * 2 + 1 - xh)
    project(1, bo)
    project(1, bp)
    b_wait(1, 1)
    b_start(1, 5)
    b_wait(1, 2)
    b_start(1, 6)
    project(1, down * 2 + xh)
    project(1, up * 2 + xh)
    b_wait(0, 5, 6)
    project(0, far * 2 + xh)
    b_wait(0, 7, 8)
    project(0, far * 2 + 1 - xh)
    b_wait(1, 3)
    b_start(1, 7)
    b_wait(1, 4)
    b_start(1, 8)
    project(1, down * 2 + 1 - xh)
    project(1, up * 2 + 1 - xh)
    b_wait(1, 5, 6)
    project(1, far * 2 + xh)
    shift(0, cs, cn).wait()
    shift(1, qs, qn).wait()
    keep = lax.broadcasted_iota(jnp.int32, (STRETCH, FEAT), 0) == 0
    more = s < SEQ - 1
    for buf, landing in ((qs, qn), (cs, cn)):
        mine = buf[192:256, :].astype(F32)
        theirs = jnp.where(more, landing[...].astype(F32), 0.0)
        buf[192:256, :] = jnp.where(keep, mine, theirs).astype(BF16)
    b_wait(1, 7, 8)
    project(1, far * 2 + 1 - xh)

    scale = HD ** (-0.5)
    left = lax.broadcasted_iota(jnp.int32, (STRETCH, 2 * HD), 1) < HD

    def pair_rows(v):
        zero = jnp.zeros_like(v)
        return jnp.concatenate([jnp.where(left, v, zero), jnp.where(left, zero, v)], axis=0)

    def attend(u, carry):
        rows = pl.ds(pl.multiple_of(u * STRETCH, STRETCH), STRETCH)
        for hp in range(2):
            lanes = slice(hp * 256, hp * 256 + 256)
            vlanes = slice(FEAT + hp * 256, FEAT + hp * 256 + 256)
            qb = pair_rows(qs[rows, lanes])
            db_ = pair_rows(cs[rows, lanes])
            kk = kv[u, :, lanes]
            vv = kv[u, :, vlanes]
            sc = dot_nt(kk, qb) * scale
            w = jnp.exp(sc - jnp.max(sc, axis=0, keepdims=True))
            p = w * (1.0 / jnp.sum(w, axis=0, keepdims=True))
            rounded = p.astype(BF16)
            dp = dot_nt(vv, db_)
            centre = jnp.sum(p * dp, axis=0, keepdims=True)
            ds = (p * (dp - centre)).astype(BF16)
            o = dot_tn(rounded, vv)
            obuf[rows, lanes] = jnp.where(left, o[:STRETCH], o[STRETCH:]).astype(BF16)
            kg = (dot(ds, qb) * scale).astype(BF16)
            vg = dot(rounded, db_).astype(BF16)
            at = pl.ds(pl.multiple_of(u * 32, 32), 32)
            for b in range(8):
                kgv[b, at, lanes] = kg[b * 32:(b + 1) * 32]
                kgv[b, at, vlanes] = vg[b * 32:(b + 1) * 32]
        return carry

    lax.fori_loop(0, 4, attend, 0)

    o_back = remote(obuf.at[pl.ds(192, 64)], on, q_ss.at[2], q_rs.at[2], dev_next)
    o_back.start()

    def term(c, b):
        lo, n = CHUNKS[c]
        return dot_nt(kgv[b], w2[lo:lo + n, :])

    def c_copy(c, k):
        ss, rs = c_ss.at[c, k], c_rs.at[c, k]
        if k == 8:
            return remote(tx[c], cx[c], ss, rs, dev_x)
        h, way = (k % 4) // 2, k % 2
        dev = dev_down if way else dev_up
        if k < 4:
            return remote(
                ta[c].at[h, pl.ds(way * HALF, HALF)], ca[c].at[h, pl.ds(way * HALF, HALF)], ss, rs, dev
            )
        return remote(tb[c].at[h, way], cb[c].at[h, way], ss, rs, dev)

    def pick(h):
        return 1 - xh if h == 0 else xh

    def c_far(c, h):
        ta[c][h] = term(c, far * 2 + pick(h)).astype(BF16)
        c_copy(c, 2 * h).start()
        c_copy(c, 2 * h + 1).start()

    def c_near(c, h):
        v = term(c, up * 2 + pick(h))
        tb[c][h, 0, HALF:] = v[HALF:].astype(BF16)
        c_copy(c, 2 * h).wait_recv()
        tb[c][h, 0, :HALF] = (v[:HALF] + ca[c][h, :HALF].astype(F32)).astype(BF16)
        c_copy(c, 4 + 2 * h).start()
        v = term(c, down * 2 + pick(h))
        tb[c][h, 1, :HALF] = v[:HALF].astype(BF16)
        c_copy(c, 2 * h + 1).wait_recv()
        tb[c][h, 1, HALF:] = (v[HALF:] + ca[c][h, HALF:].astype(F32)).astype(BF16)
        c_copy(c, 5 + 2 * h).start()

    def c_sum(c, h):
        v = term(c, y * 2 + pick(h))
        c_copy(c, 4 + 2 * h).wait_recv()
        c_copy(c, 5 + 2 * h).wait_recv()
        v = v + cb[c][h, 0].astype(F32) + cb[c][h, 1].astype(F32)
        if h == 0:
            tx[c][...] = v.astype(BF16)
            c_copy(c, 8).start()
        else:
            c_copy(c, 8).wait_recv()
            v = v + cx[c][...].astype(F32)
            fin[c][...] = v.astype(BF16).reshape(SLOTS, PIECE, CHUNKS[c][1])

    def d_do(c, act):
        exchange(sd, rd, d_ss, d_rs, c, t_minus, t_plus, act)

    def d_send(c):
        def step(q, carry):
            sd[c][q] = fin[c][slot_tab[0, q]]
            return carry

        lax.fori_loop(0, 2 * GROUPS, step, 0)
        rd[c][pl.ds(2 * me, 2)] = sd[c][pl.ds(2 * me, 2)]
        d_do(c, start)

    c_far(0, 0)
    c_far(0, 1)
    c_far(1, 0)
    c_near(0, 0)
    c_near(0, 1)
    c_far(1, 1)
    c_sum(0, 0)
    c_near(1, 0)
    c_near(1, 1)
    c_sum(0, 1)
    d_send(0)
    c_sum(1, 0)
    c_sum(1, 1)
    d_send(1)

    o_back.wait()
    edge = jnp.where(s > 0, on[...].astype(F32), 0.0)
    tail = jnp.where(keep, obuf[192:256, :].astype(F32), edge)
    whole = jnp.concatenate([obuf[0:192, :].astype(F32), tail], axis=0)
    att_out[...] = pltpu.roll(whole, STRETCH - 1, 0).astype(BF16)

    for c in range(2):
        lo, n = CHUNKS[c]
        d_do(c, wait_recv)
        rgrad[:, lo:lo + n] = dot(onehot[...], rd[c][...].reshape(2 * GROUPS * PIECE, n))
    upstream = rgrad[...].astype(BF16)
    normed[...] = upstream
    dnorm[...] = jnp.zeros_like(dnorm)

    def back(c, carry):
        cols = pl.ds(pl.multiple_of(c * 256, 256), 256)
        d_act = dot_nt(normed[...], wout[cols, :])
        d_pre = (d_act * gd[:, cols]).astype(BF16)
        dnorm[...] += dot_nt(d_pre, win[:, cols])
        return carry

    lax.fori_loop(0, FFN // 256, back, 0)
    scaled = dnorm[...] * gain[...]
    xv = db[...].reshape(TOK, WIDTH).astype(F32)
    inv = inv_s[:, 0:1]
    mean = jnp.mean(scaled * xv, axis=-1, keepdims=True)
    out = rgrad[...] + inv * scaled - xv * (inv * inv * inv * mean)
    grad_out[...] = out.astype(BF16).reshape(ROWS, PIECE, WIDTH)

    each_same(ids_same, wait_send)
    each_cross(ids_cross, wait_send)
    for c in range(2):
        a_do(c, wait_send)
        d_do(c, wait_send)
        for k in range(9):
            b_copy(c, k).wait_send()
            c_copy(c, k).wait_send()


def body(hidden, w_query, w_key, w_value, enc_gain, w_in, w_out, db_states, neighbours, d_attended):
    hbm = pl.BlockSpec(memory_space=pl.ANY)
    vmem = pl.BlockSpec(memory_space=pltpu.VMEM)
    smem = pl.BlockSpec(memory_space=pltpu.SMEM)
    dma = pltpu.SemaphoreType.DMA
    vm = pltpu.VMEM
    n0, n1 = CHUNKS[0][1], CHUNKS[1][1]

    def both(*shape, dtype=BF16):
        return [vm(shape + (n0,), dtype), vm(shape + (n1,), dtype)]

    scratch = [
        pltpu.SMEM((GROUPS, 128), jnp.int32),
        pltpu.SMEM((3, GROUPS), jnp.int32),
        pltpu.SMEM((1, SLOTS), jnp.int32),
        pltpu.SMEM((1, 2 * GROUPS), jnp.int32),
        vm((ROWS, PIECE, WIDTH), BF16),
        vm((WIDTH, FFN), BF16),
        vm((FFN, WIDTH), BF16),
        vm((WIDTH, 2 * FEAT), BF16),
        vm((TOK, DM), BF16),
        vm((DM, FEAT), BF16),
        vm((TOK, FEAT), BF16),
        vm((TOK, WIDTH), BF16),
        vm((TOK, FFN), BF16),
        vm((TOK, FFN), F32),
        vm((TOK, 128), F32),
        vm((TOK, 512), BF16),
        vm((TOK, FEAT), F32),
        vm((TOK, FEAT), BF16),
        vm((TOK, FEAT), BF16),
        vm((STRETCH, FEAT), BF16),
        vm((STRETCH, FEAT), BF16),
        vm((TOK, FEAT), BF16),
        vm((STRETCH, FEAT), BF16),
        *both(ROWS, PIECE),
        *both(2 * GROUPS, PIECE),
        *both(2 * GROUPS, PIECE),
        *both(8, BLOCK),
        vm((8, BLOCK, 2 * FEAT), F32),
        vm((4, 256, 2 * FEAT), BF16),
        vm((8, BLOCK, 2 * FEAT), BF16),
        *both(2, BLOCK),
        *both(2, 2, BLOCK),
        *both(BLOCK),
        *both(2, BLOCK),
        *both(2, 2, BLOCK),
        *both(BLOCK),
        *both(SLOTS, PIECE),
        *both(2 * GROUPS, PIECE),
        *both(2 * GROUPS, PIECE),
        vm((TOK, WIDTH), F32),
        vm((TOK, WIDTH), F32),
        dma((16,)),
        dma((16,)), dma((16,)),
        dma((2, 24)), dma((2, 24)),
        dma((2, 24)), dma((2, 24)),
        dma((2, 9)), dma((2, 9)),
        dma((2, 9)), dma((2, 9)),
        dma((3,)), dma((3,)),
    ]
    return pl.pallas_call(
        kernel,
        name="neighbour_attention",
        out_shape=(
            jax.ShapeDtypeStruct((TOK, FEAT), BF16),
            jax.ShapeDtypeStruct((ROWS, PIECE, WIDTH), BF16),
        ),
        in_specs=[smem, hbm, hbm, hbm, hbm, hbm, vmem, hbm, hbm, hbm],
        out_specs=(vmem, vmem),
        scratch_shapes=scratch,
        compiler_params=pltpu.CompilerParams(
            collective_id=0, has_side_effects=True, vmem_limit_bytes=56 * 1024 * 1024
        ),
    )(
        neighbours, db_states, hidden, w_query, w_key, w_value,
        enc_gain.reshape(1, WIDTH), w_in, w_out, d_attended,
    )


def solution(mesh):
    in_specs = (
        P(("role", "seq"), None),
        P(None, "tp"),
        P(None, "tp"),
        P(None, "tp"),
        P(),
        P(),
        P(),
        P(("role", "seq"), "tp", None),
        P(("role", "seq"), None),
        P(("role", "seq"), "tp"),
    )
    out_specs = (P(("role", "seq"), "tp"), P(("role", "seq"), "tp", None))
    return jax.shard_map(body, mesh=mesh, in_specs=in_specs, out_specs=out_specs, check_vma=False)
```

```python
import jax
import jax.numpy as jnp
from jax import lax
from jax.experimental import pallas as pl
from jax.experimental.pallas import tpu as pltpu
from jax.sharding import PartitionSpec as P

HD = 128
STRETCH = 64
EPS = 1e-06
MESH = pl.DeviceIdType.MESH
BF16 = jnp.bfloat16
F32 = jnp.float32
GELU_A = 0.7978845608028654
GELU_B = 0.044715

GROUPS = 16
SEQ = 8
ROWS = 16
SLOTS = 8
PIECE = 16
WIDTH = 896
FFN = 1792
TOK = 256
DM = 8192
FEAT = 512
BLOCK = SLOTS * PIECE
HALF = BLOCK // 2
CHUNKS = ((0, 384), (384, 512))
QK = 1024
QSTEPS = DM // QK


def dot(a, b):
    return jnp.dot(a, b, preferred_element_type=F32)


def dot_nt(a, b):
    return lax.dot_general(a, b, (((1,), (1,)), ((), ())), preferred_element_type=F32)


def dot_tn(a, b):
    return lax.dot_general(a, b, (((0,), (0,)), ((), ())), preferred_element_type=F32)


def kernel(
    nb, db_hbm, hid_hbm, wq_hbm, wk_hbm, wv_hbm, gain, win_hbm, wout_hbm, cot_hbm,
    att_out, grad_out,
    ids, row_tab, own_tab, slot_tab,
    db, win, wout, w2, w2t, hid, wq, cot,
    normed, active, gd, inv_s, onehot, qacc, qs, cs, qn, cn, obuf, on,
    enc0, enc1, sa0, sa1, ra0, ra1, g0, g1, kvacc, kv, kgv,
    ca0, ca1, cb0, cb1, cx0, cx1, ta0, ta1, tb0, tb1, tx0, tx1, th0, th1,
    fin0, fin1, sd0, sd1, rd0, rd1, rgrad, dnorm,
    lsem, ids_ss, ids_rs, a_ss, a_rs, d_ss, d_rs, b_ss, b_rs, c_ss, c_rs, q_ss, q_rs,
):
    enc, sa, ra, g = (enc0, enc1), (sa0, sa1), (ra0, ra1), (g0, g1)
    ca, cb, cx = (ca0, ca1), (cb0, cb1), (cx0, cx1)
    ta, tb, tx, th = (ta0, ta1), (tb0, tb1), (tx0, tx1), (th0, th1)
    fin, sd, rd = (fin0, fin1), (sd0, sd1), (rd0, rd1)
    r = lax.axis_index("role")
    s = lax.axis_index("seq")
    t = lax.axis_index("tp")
    y = t // 2
    xh = t % 2
    me = r * SEQ + s
    up = (y + 1) % 4
    down = (y + 3) % 4
    far = (y + 2) % 4
    dev_up = (r, s, up * 2 + xh)
    dev_down = (r, s, down * 2 + xh)
    dev_x = (r, s, y * 2 + 1 - xh)
    dev_next = (r, (s + 1) % SEQ, t)
    dev_prev = (r, (s + SEQ - 1) % SEQ, t)

    def remote(src, dst, ss, rs, dev):
        return pltpu.make_async_remote_copy(
            src_ref=src, dst_ref=dst, send_sem=ss, recv_sem=rs, device_id=dev, device_id_type=MESH
        )

    barrier = pltpu.get_barrier_semaphore()

    def greet(dev):
        pl.semaphore_signal(barrier, inc=1, device_id=dev, device_id_type=MESH)

    def peer(j):
        q = (me + j) % GROUPS
        return q, (q // SEQ, q % SEQ, t)

    def greet_group(j, c):
        greet(peer(j)[1])
        return c

    lax.fori_loop(1, GROUPS, greet_group, 0)
    greet(dev_up)
    greet(dev_down)
    greet(dev_x)

    loads = []

    def load(src, dst):
        cp = pltpu.make_async_copy(src, dst, lsem.at[len(loads)])
        cp.start()
        loads.append(cp)
        return cp

    l_db = load(db_hbm, db)
    l_win = load(win_hbm, win)
    l_wout = load(wout_hbm, wout)
    l_cot = load(cot_hbm, cot)
    l_hid = load(hid_hbm, hid)
    l_wq = [
        load(wq_hbm.at[pl.ds(i * QK, QK)], wq.at[pl.ds(i * QK, QK)]) for i in range(QSTEPS)
    ]
    l_wk = load(wk_hbm, w2.at[:, pl.ds(0, FEAT)])
    l_wv = load(wv_hbm, w2.at[:, pl.ds(FEAT, FEAT)])

    def copy_ids(i, c):
        ids[me, i] = nb[i % 2, i // 2]
        return c

    lax.fori_loop(0, SLOTS, copy_ids, 0)

    pl.semaphore_wait(barrier, 18)

    def each(make, act):
        def step(j, c):
            act(make(j))
            return c

        lax.fori_loop(1, GROUPS, step, 0)

    def ids_copy(j):
        return remote(ids.at[me], ids.at[me], ids_ss.at[j], ids_rs.at[j], peer(j)[1])

    start = lambda cp: cp.start()
    wait_recv = lambda cp: cp.wait_recv()
    wait_send = lambda cp: cp.wait_send()

    each(ids_copy, start)

    l_db.wait()
    xv = db[...].reshape(TOK, WIDTH).astype(F32)
    inverse = lax.rsqrt(jnp.mean(xv * xv, axis=-1, keepdims=True) + EPS)
    inv_s[...] = jnp.broadcast_to(inverse, (TOK, 128))
    gain_row = gain[...].reshape(1, WIDTH)
    normed[...] = (xv * inverse * gain_row).astype(BF16)
    l_win.wait()

    def first_layer(c, carry):
        cols = pl.ds(pl.multiple_of(c * 256, 256), 256)
        pre = dot(normed[...], win[:, cols])
        sq = pre * pre
        th = jnp.tanh(GELU_A * (pre + GELU_B * (sq * pre)))
        cdf = 0.5 * (1.0 + th)
        active[:, cols] = (pre * cdf).astype(BF16)
        gd[:, cols] = cdf + pre * (0.5 * GELU_A) * (1.0 - th * th) * (1.0 + 3.0 * GELU_B * sq)
        return carry

    lax.fori_loop(0, FFN // 256, first_layer, 0)
    l_wout.wait()

    def encode(c):
        lo, n = CHUNKS[c]
        rows = db[:, :, lo:lo + n].reshape(TOK, n).astype(F32)
        out = rows + dot(active[...], wout[:, lo:lo + n])
        enc[c][...] = out.astype(BF16).reshape(ROWS, PIECE, n)

    encode(0)

    each(ids_copy, wait_recv)

    def row_step(q, c):
        cnt = jnp.int32(0)
        row0 = jnp.int32(0)
        row1 = jnp.int32(0)
        for k in range(SLOTS):
            v = ids[q, k] - me * ROWS
            hit = (v >= 0) & (v < ROWS)
            row0 = jnp.where(hit & (cnt == 0), v, row0)
            row1 = jnp.where(hit & (cnt == 1), v, row1)
            cnt = cnt + hit.astype(jnp.int32)
        row_tab[0, q] = row0
        row_tab[1, q] = row1
        row_tab[2, q] = cnt
        return c

    lax.fori_loop(0, GROUPS, row_step, 0)

    def fill(c):
        def step(q, carry):
            sa[c][2 * q] = enc[c][row_tab[0, q]]
            sa[c][2 * q + 1] = enc[c][row_tab[1, q]]
            return carry

        lax.fori_loop(0, GROUPS, step, 0)
        ra[c][pl.ds(2 * me, 2)] = sa[c][pl.ds(2 * me, 2)]

    def exchange(src, dst, ss, rs, c):
        def make(j):
            q, dev = peer(j)
            return remote(
                src[c].at[pl.ds(2 * q, 2)], dst[c].at[pl.ds(2 * me, 2)], ss.at[c, j], rs.at[c, j], dev
            )

        return make

    a_copy = [exchange(sa, ra, a_ss, a_rs, c) for c in range(2)]
    d_copy = [exchange(sd, rd, d_ss, d_rs, c) for c in range(2)]

    fill(0)
    each(a_copy[0], start)
    encode(1)
    fill(1)

    def own_step(k, c):
        v = ids[me, k]
        owner = v // ROWS
        rank = jnp.int32(0)
        for e in range(SLOTS):
            same = (ids[me, e] // ROWS == owner) & (e < k)
            rank = rank + same.astype(jnp.int32)
        own_tab[0, k] = owner * 2 + rank
        return c

    lax.fori_loop(0, SLOTS, own_step, 0)

    def slot_step(q, c):
        slot = jnp.int32(0)
        for k in range(SLOTS):
            slot = jnp.where(own_tab[0, k] == q, k, slot)
        slot_tab[0, q] = slot
        return c

    lax.fori_loop(0, 2 * GROUPS, slot_step, 0)

    def shift(k, buf, landing):
        return remote(buf.at[pl.ds(192, 64)], landing, q_ss.at[k], q_rs.at[k], dev_prev)

    l_cot.wait()
    cs[...] = pltpu.roll(cot[...].astype(F32), TOK - (STRETCH - 1), 0).astype(BF16)
    shift(0, cs, cn).start()
    l_hid.wait()

    def query_step(i):
        l_wq[i].wait()
        part = dot(hid[:, i * QK:(i + 1) * QK], wq[pl.ds(i * QK, QK), :])
        if i == 0:
            qacc[...] = part
        else:
            qacc[...] += part

    def query_end():
        turned = pltpu.roll(qacc[...].astype(BF16).astype(F32), TOK - (STRETCH - 1), 0)
        qs[...] = turned.astype(BF16)
        shift(1, qs, qn).start()

    def build_selection():
        lane_k = lax.broadcasted_iota(jnp.int32, (8, 512), 1) // PIECE

        def col_step(q, cols):
            cnt = row_tab[2, q]
            first = jnp.where(cnt > 0, row_tab[0, q], -1)
            second = jnp.where(cnt > 1, row_tab[1, q], -1)
            cols = jnp.where(lane_k == 2 * q, first, cols)
            return jnp.where(lane_k == 2 * q + 1, second, cols)

        cols = lax.fori_loop(0, GROUPS, col_step, jnp.full((8, 512), -1, jnp.int32))
        row_i = lax.broadcasted_iota(jnp.int32, (TOK, 512), 0)
        col_i = lax.broadcasted_iota(jnp.int32, (TOK, 512), 1)
        match = (row_i // PIECE == cols[0:1, :]) & (row_i % PIECE == col_i % PIECE)
        onehot[...] = jnp.where(match, 1.0, 0.0).astype(BF16)

    for i in range(3):
        query_step(i)

    def follow(j, c):
        a_copy[0](j).wait_send()
        a_copy[1](j).start()
        return c

    lax.fori_loop(1, GROUPS, follow, 0)
    each(ids_copy, wait_send)

    bo = t
    bp = y * 2 + 1 - xh

    def b_copy(c, k):
        ss, rs = b_ss.at[c, k], b_rs.at[c, k]
        half = (0, 1, 0, 1, 1, 0, 0, 1, 1, 0, 0, 1, 0, 1)[k]
        if k < 2:
            b, dev = bo, dev_x
        elif k < 10:
            b = bo if k < 6 else bp
            dev = dev_up if (k - 2) % 4 < 2 else dev_down
        else:
            h = xh if k < 12 else 1 - xh
            b, dev = (down * 2 + h, dev_up) if half == 0 else (up * 2 + h, dev_down)
        part = g[c].at[b, pl.ds(half * HALF, HALF)]
        return remote(part, part, ss, rs, dev)

    def select(c):
        def step(k, carry):
            n = CHUNKS[c][1]
            g[c][bo, pl.ds(pl.multiple_of(k * PIECE, PIECE), PIECE)] = ra[c][own_tab[0, k]]
            return carry

        lax.fori_loop(0, SLOTS, step, 0)

    def project(c, b):
        lo, n = CHUNKS[c]
        part = dot(g[c][b], w2[lo:lo + n, :])
        if c == 0:
            kvacc[b] = part
        else:
            out = (kvacc[b] + part).astype(BF16)
            for u in range(4):
                kv[u, pl.ds(pl.multiple_of(b * 32, 32), 32), :] = out[u * 32:(u + 1) * 32]

    def b_wait(c, *ks):
        for k in ks:
            b_copy(c, k).wait_recv()

    def b_start(c, *ks):
        for k in ks:
            b_copy(c, k).start()

    def begin(c):
        each(a_copy[c], wait_recv)
        select(c)
        b_start(c, 0, 2, 4, 1, 3, 5)

    def first_relays(c):
        b_wait(c, 2)
        b_start(c, 10)
        b_wait(c, 4)
        b_start(c, 11)

    def partner_sends(c):
        b_wait(c, 0)
        b_start(c, 6)
        b_wait(c, 1)
        b_start(c, 8, 7, 9)

    def second_relays(c):
        b_wait(c, 6)
        b_start(c, 12)
        b_wait(c, 8)
        b_start(c, 13)

    l_wk.wait()
    l_wv.wait()
    query_step(3)
    query_step(4)
    begin(0)
    project(0, bo)
    query_step(5)
    query_step(6)
    first_relays(0)
    partner_sends(0)
    project(0, bp)
    query_step(7)
    query_end()
    begin(1)
    second_relays(0)
    b_wait(0, 3, 5)
    project(0, down * 2 + xh)
    project(0, up * 2 + xh)
    first_relays(1)
    partner_sends(1)
    project(1, bo)
    project(1, bp)
    build_selection()
    for lo in range(0, WIDTH, 128):
        w2t[:, lo:lo + 128] = w2[lo:lo + 128, :].T
    b_wait(0, 7, 9)
    project(0, down * 2 + 1 - xh)
    project(0, up * 2 + 1 - xh)
    b_wait(0, 10, 11)
    project(0, far * 2 + xh)
    b_wait(0, 12, 13)
    project(0, far * 2 + 1 - xh)
    second_relays(1)
    b_wait(1, 3, 5)
    project(1, down * 2 + xh)
    project(1, up * 2 + xh)
    each(a_copy[1], wait_send)
    shift(0, cs, cn).wait()
    shift(1, qs, qn).wait()
    keep = lax.broadcasted_iota(jnp.int32, (STRETCH, FEAT), 0) == 0
    more = s < SEQ - 1
    for buf, landing in ((qs, qn), (cs, cn)):
        mine = buf[192:256, :].astype(F32)
        theirs = jnp.where(more, landing[...].astype(F32), 0.0)
        buf[192:256, :] = jnp.where(keep, mine, theirs).astype(BF16)
    b_wait(1, 7, 9)
    project(1, down * 2 + 1 - xh)
    project(1, up * 2 + 1 - xh)
    b_wait(1, 10, 11)
    project(1, far * 2 + xh)
    b_wait(1, 12, 13)
    project(1, far * 2 + 1 - xh)

    scale = HD ** (-0.5)
    left = lax.broadcasted_iota(jnp.int32, (STRETCH, 2 * HD), 1) < HD

    def pair_rows(v):
        zero = jnp.zeros_like(v)
        return jnp.concatenate([jnp.where(left, v, zero), jnp.where(left, zero, v)], axis=0)

    for u in range(4):
        rows = slice(u * STRETCH, u * STRETCH + STRETCH)
        for hp in range(2):
            lanes = slice(hp * 256, hp * 256 + 256)
            vlanes = slice(FEAT + hp * 256, FEAT + hp * 256 + 256)
            qb = pair_rows(qs[rows, lanes])
            db_ = pair_rows(cs[rows, lanes])
            kk = kv[u, :, lanes]
            vv = kv[u, :, vlanes]
            sc = dot_nt(kk, qb) * scale
            w = jnp.exp(sc - jnp.max(sc, axis=0, keepdims=True))
            p = w * (1.0 / jnp.sum(w, axis=0, keepdims=True))
            rounded = p.astype(BF16)
            dp = dot_nt(vv, db_)
            centre = jnp.sum(p * dp, axis=0, keepdims=True)
            ds = (p * (dp - centre)).astype(BF16)
            o = dot_tn(rounded, vv)
            obuf[rows, lanes] = jnp.where(left, o[:STRETCH], o[STRETCH:]).astype(BF16)
            kg = (dot(ds, qb) * scale).astype(BF16)
            vg = dot(rounded, db_).astype(BF16)
            at = slice(u * 32, u * 32 + 32)
            for b in range(8):
                kgv[b, at, lanes] = kg[b * 32:(b + 1) * 32]
                kgv[b, at, vlanes] = vg[b * 32:(b + 1) * 32]

    o_back = remote(obuf.at[pl.ds(192, 64)], on, q_ss.at[2], q_rs.at[2], dev_next)
    o_back.start()

    def term(c, b):
        lo, n = CHUNKS[c]
        return dot(kgv[b], w2t[:, lo:lo + n])

    def c_copy(c, k):
        ss, rs = c_ss.at[c, k], c_rs.at[c, k]
        if k >= 12:
            part = pl.ds((k - 12) * HALF, HALF)
            return remote(tx[c].at[part], cx[c].at[part], ss, rs, dev_x)
        h, kind, way = k // 6, (k % 6) // 2, k % 2
        dev = dev_down if way else dev_up
        half = 1 - way if kind == 1 else way
        part = pl.ds(half * HALF, HALF)
        if kind == 0:
            return remote(ta[c].at[h, part], ca[c].at[h, part], ss, rs, dev)
        return remote(tb[c].at[h, way, part], cb[c].at[h, way, part], ss, rs, dev)

    def c_start(c, *ks):
        for k in ks:
            c_copy(c, k).start()

    def pick(h):
        return 1 - xh if h == 0 else xh

    def c_sent(c, *ks):
        for k in ks:
            c_copy(c, k).wait_send()

    def c_far(c, h):
        ta[c][h] = term(c, far * 2 + pick(h)).astype(BF16)

    def c_near(c, h):
        v = term(c, up * 2 + pick(h))
        tb[c][h, 0, HALF:] = v[HALF:].astype(BF16)
        th[c][h, 0] = v[:HALF]
        v = term(c, down * 2 + pick(h))
        tb[c][h, 1, :HALF] = v[:HALF].astype(BF16)
        th[c][h, 1] = v[HALF:]

    def c_merge(c, h):
        c_copy(c, 6 * h).wait_recv()
        tb[c][h, 0, :HALF] = (th[c][h, 0] + ca[c][h, :HALF].astype(F32)).astype(BF16)
        c_copy(c, 6 * h + 1).wait_recv()
        tb[c][h, 1, HALF:] = (th[c][h, 1] + ca[c][h, HALF:].astype(F32)).astype(BF16)

    def c_sum(c, h):
        v = term(c, y * 2 + pick(h))
        for k in (2, 3, 4, 5):
            c_copy(c, 6 * h + k).wait_recv()
        v = v + cb[c][h, 0].astype(F32) + cb[c][h, 1].astype(F32)
        if h == 0:
            tx[c][...] = v.astype(BF16)
            c_start(c, 12, 13)
        else:
            c_copy(c, 12).wait_recv()
            c_copy(c, 13).wait_recv()
            v = v + cx[c][...].astype(F32)
            fin[c][...] = v.astype(BF16).reshape(SLOTS, PIECE, CHUNKS[c][1])

    def d_send(c):
        def step(q, carry):
            sd[c][q] = fin[c][slot_tab[0, q]]
            return carry

        lax.fori_loop(0, 2 * GROUPS, step, 0)
        rd[c][pl.ds(2 * me, 2)] = sd[c][pl.ds(2 * me, 2)]
        each(d_copy[c], start)

    c_far(1, 0)
    c_start(1, 0, 1)
    c_far(1, 1)
    c_start(1, 6, 7)
    c_near(1, 0)
    c_sent(1, 0, 1)
    c_start(1, 2, 3)
    c_merge(1, 0)
    c_sent(1, 6, 7)
    c_start(1, 4, 5)
    c_near(1, 1)
    c_sent(1, 2, 3)
    c_start(1, 8, 9)
    c_merge(1, 1)
    c_sent(1, 4, 5)
    c_start(1, 10, 11)
    c_far(0, 0)
    c_sent(1, 8, 9)
    c_start(0, 0, 1)
    c_sum(1, 0)
    c_far(0, 1)
    c_sent(1, 10, 11)
    c_start(0, 6, 7)
    c_near(0, 0)
    c_sent(0, 0, 1)
    c_start(0, 2, 3)
    c_merge(0, 0)
    c_sent(0, 6, 7)
    c_start(0, 4, 5)
    c_near(0, 1)
    c_sent(0, 2, 3)
    c_start(0, 8, 9)
    c_sum(1, 1)
    d_send(1)
    c_merge(0, 1)
    c_sent(0, 4, 5)
    c_start(0, 10, 11)
    c_sum(0, 0)
    c_sum(0, 1)
    d_send(0)

    o_back.wait()
    edge = jnp.where(s > 0, on[...].astype(F32), 0.0)
    tail = jnp.where(keep, obuf[192:256, :].astype(F32), edge)
    whole = jnp.concatenate([obuf[0:192, :].astype(F32), tail], axis=0)
    att_out[...] = pltpu.roll(whole, STRETCH - 1, 0).astype(BF16)

    for c in range(2):
        for k in range(14):
            b_copy(c, k).wait_send()
    c_sent(0, 8, 9, 10, 11, 12, 13)
    c_sent(1, 12, 13)
    each(d_copy[1], wait_send)

    for c in (1, 0):
        lo, n = CHUNKS[c]
        each(d_copy[c], wait_recv)
        rg = dot(onehot[...], rd[c][...].reshape(2 * GROUPS * PIECE, n))
        rgrad[:, lo:lo + n] = rg
        normed[:, lo:lo + n] = rg.astype(BF16)
    for lo in range(0, FFN, 256):
        d_act = dot_nt(normed[...], wout[lo:lo + 256, :])
        active[:, lo:lo + 256] = (d_act * gd[:, lo:lo + 256]).astype(BF16)
    mean = jnp.zeros((TOK, 1), F32)
    for lo, n in CHUNKS:
        part = dot_nt(active[...], win[lo:lo + n, :]) * gain_row[:, lo:lo + n]
        dnorm[:, lo:lo + n] = part
        rows = db[:, :, lo:lo + n].reshape(TOK, n).astype(F32)
        mean = mean + jnp.sum(part * rows, axis=-1, keepdims=True)
    inv = inv_s[:, 0:1]
    xv = db[...].reshape(TOK, WIDTH).astype(F32)
    cubed = inv * inv * inv * (mean * (1.0 / WIDTH))
    out = rgrad[...] + inv * dnorm[...] - xv * cubed
    grad_out[...] = out.astype(BF16).reshape(ROWS, PIECE, WIDTH)
    each(d_copy[0], wait_send)


def finish(att_ref, grad_ref, att_out, grad_out, sem):
    one = pltpu.make_async_copy(att_ref, att_out, sem.at[0])
    two = pltpu.make_async_copy(grad_ref, grad_out, sem.at[1])
    one.start()
    two.start()
    one.wait()
    two.wait()


def body(hidden, w_query, w_key, w_value, enc_gain, w_in, w_out, db_states, neighbours, d_attended):
    hbm = pl.BlockSpec(memory_space=pl.ANY)
    vmem = pl.BlockSpec(memory_space=pltpu.VMEM)
    smem = pl.BlockSpec(memory_space=pltpu.SMEM)
    dma = pltpu.SemaphoreType.DMA
    vm = pltpu.VMEM
    n0, n1 = CHUNKS[0][1], CHUNKS[1][1]

    def both(*shape, dtype=BF16):
        return [vm(shape + (n0,), dtype), vm(shape + (n1,), dtype)]

    scratch = [
        pltpu.SMEM((GROUPS, 128), jnp.int32),
        pltpu.SMEM((3, GROUPS), jnp.int32),
        pltpu.SMEM((1, SLOTS), jnp.int32),
        pltpu.SMEM((1, 2 * GROUPS), jnp.int32),
        vm((ROWS, PIECE, WIDTH), BF16),
        vm((WIDTH, FFN), BF16),
        vm((FFN, WIDTH), BF16),
        vm((WIDTH, 2 * FEAT), BF16),
        vm((2 * FEAT, WIDTH), BF16),
        vm((TOK, DM), BF16),
        vm((DM, FEAT), BF16),
        vm((TOK, FEAT), BF16),
        vm((TOK, WIDTH), BF16),
        vm((TOK, FFN), BF16),
        vm((TOK, FFN), F32),
        vm((TOK, 128), F32),
        vm((TOK, 512), BF16),
        vm((TOK, FEAT), F32),
        vm((TOK, FEAT), BF16),
        vm((TOK, FEAT), BF16),
        vm((STRETCH, FEAT), BF16),
        vm((STRETCH, FEAT), BF16),
        vm((TOK, FEAT), BF16),
        vm((STRETCH, FEAT), BF16),
        *both(ROWS, PIECE),
        *both(2 * GROUPS, PIECE),
        *both(2 * GROUPS, PIECE),
        *both(8, BLOCK),
        vm((8, BLOCK, 2 * FEAT), F32),
        vm((4, 256, 2 * FEAT), BF16),
        vm((8, BLOCK, 2 * FEAT), BF16),
        *both(2, BLOCK),
        *both(2, 2, BLOCK),
        *both(BLOCK),
        *both(2, BLOCK),
        *both(2, 2, BLOCK),
        *both(BLOCK),
        *both(2, 2, HALF, dtype=F32),
        *both(SLOTS, PIECE),
        *both(2 * GROUPS, PIECE),
        *both(2 * GROUPS, PIECE),
        vm((TOK, WIDTH), F32),
        vm((TOK, WIDTH), F32),
        dma((16,)),
        dma((16,)), dma((16,)),
        dma((2, 16)), dma((2, 16)),
        dma((2, 16)), dma((2, 16)),
        dma((2, 14)), dma((2, 14)),
        dma((2, 14)), dma((2, 14)),
        dma((3,)), dma((3,)),
    ]
    att, grad = pl.pallas_call(
        kernel,
        name="neighbour_attention",
        out_shape=(
            jax.ShapeDtypeStruct((TOK, FEAT), BF16),
            jax.ShapeDtypeStruct((ROWS, PIECE, WIDTH), BF16),
        ),
        in_specs=[smem, hbm, hbm, hbm, hbm, hbm, vmem, hbm, hbm, hbm],
        out_specs=(vmem, vmem),
        scratch_shapes=scratch,
        compiler_params=pltpu.CompilerParams(
            collective_id=0, has_side_effects=True, vmem_limit_bytes=56 * 1024 * 1024
        ),
    )(
        neighbours.T, db_states, hidden, w_query, w_key, w_value,
        enc_gain, w_in, w_out, d_attended,
    )
    return pl.pallas_call(
        finish,
        name="finish",
        out_shape=(
            jax.ShapeDtypeStruct((TOK, FEAT), BF16),
            jax.ShapeDtypeStruct((ROWS, PIECE, WIDTH), BF16),
        ),
        in_specs=[hbm, hbm],
        out_specs=(vmem, vmem),
        scratch_shapes=[dma((2,))],
    )(att, grad)


def solution(mesh):
    in_specs = (
        P(("role", "seq"), None),
        P(None, "tp"),
        P(None, "tp"),
        P(None, "tp"),
        P(),
        P(),
        P(),
        P(("role", "seq"), "tp", None),
        P(("role", "seq"), None),
        P(("role", "seq"), "tp"),
    )
    out_specs = (P(("role", "seq"), "tp"), P(("role", "seq"), "tp", None))
    return jax.shard_map(body, mesh=mesh, in_specs=in_specs, out_specs=out_specs, check_vma=False)
```

```python
import jax
import jax.numpy as jnp
from jax import lax
from jax.experimental import pallas as pl
from jax.experimental.pallas import tpu as pltpu
from jax.sharding import PartitionSpec as P

HD = 128
STRETCH = 64
EPS = 1e-06
MESH = pl.DeviceIdType.MESH
BF16 = jnp.bfloat16
F32 = jnp.float32
GELU_A = 0.7978845608028654
GELU_B = 0.044715

GROUPS = 16
SEQ = 8
ROWS = 16
SLOTS = 8
PIECE = 16
WIDTH = 896
FFN = 1792
TOK = 256
DM = 8192
FEAT = 512
BLOCK = SLOTS * PIECE
HALF = BLOCK // 2
QUARTER = BLOCK // 4
QK = 1024
QSTEPS = DM // QK


def dot(a, b):
    return jnp.dot(a, b, preferred_element_type=F32)


def dot_nt(a, b):
    return lax.dot_general(a, b, (((1,), (1,)), ((), ())), preferred_element_type=F32)


def dot_tn(a, b):
    return lax.dot_general(a, b, (((0,), (0,)), ((), ())), preferred_element_type=F32)


def kernel(
    nb, db_hbm, hid_hbm, wq_hbm, wk_hbm, wv_hbm, gain, win_hbm, wout_hbm, cot_hbm,
    att_out, grad_out,
    ids, row_tab, own_tab, slot_tab,
    db, win, wout, winT, woutT, w2, w2t, hid, wq, cot,
    normed, active, gd, inv_s, onehot, qacc, qs, cs, qn, cn, obuf, on,
    enc, sa, ra, g, kv, prob, kgv, terms,
    xb_s, xb_r, fa_s, fa_r, na_s, na_r, fb_s, fb_r, nb_s, nb_r, xa_s, xa_r,
    fin, sd, rd, rgrad, dnorm,
    lsem, ids_ss, ids_rs, a_ss, a_rs, d_ss, d_rs, b_ss, b_rs, c_ss, c_rs, q_ss, q_rs,
):
    r = lax.axis_index("role")
    s = lax.axis_index("seq")
    t = lax.axis_index("tp")
    y = t // 2
    xh = t % 2
    me = r * SEQ + s
    up = (y + 1) % 4
    down = (y + 3) % 4
    far = (y + 2) % 4
    dev_up = (r, s, up * 2 + xh)
    dev_down = (r, s, down * 2 + xh)
    dev_x = (r, s, y * 2 + 1 - xh)
    dev_next = (r, (s + 1) % SEQ, t)
    dev_prev = (r, (s + SEQ - 1) % SEQ, t)

    def remote(src, dst, ss, rs, dev):
        return pltpu.make_async_remote_copy(
            src_ref=src, dst_ref=dst, send_sem=ss, recv_sem=rs, device_id=dev, device_id_type=MESH
        )

    barrier = pltpu.get_barrier_semaphore()

    def greet(dev):
        pl.semaphore_signal(barrier, inc=1, device_id=dev, device_id_type=MESH)

    def peer(j):
        q = (me + j) % GROUPS
        return q, (q // SEQ, q % SEQ, t)

    def greet_group(j, c):
        greet(peer(j)[1])
        return c

    lax.fori_loop(1, GROUPS, greet_group, 0)
    greet(dev_up)
    greet(dev_down)
    greet(dev_x)

    loads = []

    def load(src, dst):
        cp = pltpu.make_async_copy(src, dst, lsem.at[len(loads)])
        cp.start()
        loads.append(cp)
        return cp

    l_db = load(db_hbm, db)
    l_win = load(win_hbm, win)
    l_wout = load(wout_hbm, wout)
    l_cot = load(cot_hbm, cot)
    l_hid = load(hid_hbm, hid)
    l_wq = [
        load(wq_hbm.at[pl.ds(i * QK, QK)], wq.at[pl.ds(i * QK, QK)]) for i in range(QSTEPS)
    ]
    l_wk = load(wk_hbm, w2.at[:, pl.ds(0, FEAT)])
    l_wv = load(wv_hbm, w2.at[:, pl.ds(FEAT, FEAT)])

    def copy_ids(i, c):
        ids[me, i] = nb[i % 2, i // 2]
        return c

    lax.fori_loop(0, SLOTS, copy_ids, 0)

    pl.semaphore_wait(barrier, 18)

    def each(make, act):
        def step(j, c):
            act(make(j))
            return c

        lax.fori_loop(1, GROUPS, step, 0)

    def ids_copy(j):
        return remote(ids.at[me], ids.at[me], ids_ss.at[j], ids_rs.at[j], peer(j)[1])

    start = lambda cp: cp.start()
    wait_recv = lambda cp: cp.wait_recv()
    wait_send = lambda cp: cp.wait_send()

    each(ids_copy, start)

    l_db.wait()
    xv = db[...].reshape(TOK, WIDTH).astype(F32)
    inverse = lax.rsqrt(jnp.mean(xv * xv, axis=-1, keepdims=True) + EPS)
    inv_s[...] = jnp.broadcast_to(inverse, (TOK, 128))
    gain_row = gain[...].reshape(1, WIDTH)
    normed[...] = (xv * inverse * gain_row).astype(BF16)
    l_win.wait()

    def first_layer(c, carry):
        cols = pl.ds(pl.multiple_of(c * 256, 256), 256)
        pre = dot(normed[...], win[:, cols])
        sq = pre * pre
        th = jnp.tanh(GELU_A * (pre + GELU_B * (sq * pre)))
        cdf = 0.5 * (1.0 + th)
        active[:, cols] = (pre * cdf).astype(BF16)
        gd[:, cols] = cdf + pre * (0.5 * GELU_A) * (1.0 - th * th) * (1.0 + 3.0 * GELU_B * sq)
        return carry

    lax.fori_loop(0, FFN // 256, first_layer, 0)
    l_wout.wait()

    rows = db[...].reshape(TOK, WIDTH).astype(F32)
    coded = rows + dot(active[...], wout[...])
    enc[...] = coded.astype(BF16).reshape(ROWS, PIECE, WIDTH)

    def row_step(q):
        cnt = jnp.int32(0)
        row0 = jnp.int32(0)
        row1 = jnp.int32(0)
        for k in range(SLOTS):
            v = ids[q, k] - me * ROWS
            hit = (v >= 0) & (v < ROWS)
            row0 = jnp.where(hit & (cnt == 0), v, row0)
            row1 = jnp.where(hit & (cnt == 1), v, row1)
            cnt = cnt + hit.astype(jnp.int32)
        row_tab[0, q] = row0
        row_tab[1, q] = row1
        row_tab[2, q] = cnt
        return row0, row1

    def exchange(src, dst, ss, rs):
        def make(j):
            q, dev = peer(j)
            return remote(src.at[pl.ds(2 * q, 2)], dst.at[pl.ds(2 * me, 2)], ss.at[j], rs.at[j], dev)

        return make

    a_copy = exchange(sa, ra, a_ss, a_rs)
    d_copy = exchange(sd, rd, d_ss, d_rs)

    def serve(j, c):
        ids_copy(GROUPS - j).wait_recv()
        q = (me + j) % GROUPS
        row0, row1 = row_step(q)
        sa[2 * q] = enc[row0]
        sa[2 * q + 1] = enc[row1]
        a_copy(j).start()
        return c

    lax.fori_loop(1, GROUPS, serve, 0)
    row0, row1 = row_step(me)
    ra[2 * me] = enc[row0]
    ra[2 * me + 1] = enc[row1]

    def own_step(k, c):
        v = ids[me, k]
        owner = v // ROWS
        rank = jnp.int32(0)
        for e in range(SLOTS):
            same = (ids[me, e] // ROWS == owner) & (e < k)
            rank = rank + same.astype(jnp.int32)
        own_tab[0, k] = owner * 2 + rank
        return c

    lax.fori_loop(0, SLOTS, own_step, 0)

    def slot_step(q, c):
        slot = jnp.int32(0)
        for k in range(SLOTS):
            slot = jnp.where(own_tab[0, k] == q, k, slot)
        slot_tab[0, q] = slot
        return c

    lax.fori_loop(0, 2 * GROUPS, slot_step, 0)

    def shift(k, buf, landing):
        return remote(buf.at[pl.ds(192, 64)], landing, q_ss.at[k], q_rs.at[k], dev_prev)

    l_cot.wait()
    cs[...] = pltpu.roll(cot[...].astype(F32), TOK - (STRETCH - 1), 0).astype(BF16)
    shift(0, cs, cn).start()
    l_hid.wait()

    def query_step(i):
        l_wq[i].wait()
        part = dot(hid[:, i * QK:(i + 1) * QK], wq[pl.ds(i * QK, QK), :])
        if i == 0:
            qacc[...] = part
        else:
            qacc[...] += part

    def query_end():
        turned = pltpu.roll(qacc[...].astype(BF16).astype(F32), TOK - (STRETCH - 1), 0)
        qs[...] = turned.astype(BF16)
        shift(1, qs, qn).start()

    def build_selection():
        lane_k = lax.broadcasted_iota(jnp.int32, (8, 512), 1) // PIECE

        def col_step(q, cols):
            cnt = row_tab[2, q]
            first = jnp.where(cnt > 0, row_tab[0, q], -1)
            second = jnp.where(cnt > 1, row_tab[1, q], -1)
            cols = jnp.where(lane_k == 2 * q, first, cols)
            return jnp.where(lane_k == 2 * q + 1, second, cols)

        cols = lax.fori_loop(0, GROUPS, col_step, jnp.full((8, 512), -1, jnp.int32))
        row_i = lax.broadcasted_iota(jnp.int32, (TOK, 512), 0)
        col_i = lax.broadcasted_iota(jnp.int32, (TOK, 512), 1)
        match = (row_i // PIECE == cols[0:1, :]) & (row_i % PIECE == col_i % PIECE)
        onehot[...] = jnp.where(match, 1.0, 0.0).astype(BF16)

    for i in range(QSTEPS):
        query_step(i)
    query_end()
    l_wk.wait()
    l_wv.wait()
    for lo in range(0, WIDTH, 128):
        w2t[:, lo:lo + 128] = w2[lo:lo + 128, :].T
    build_selection()
    each(ids_copy, wait_send)

    bo = t
    bp = y * 2 + 1 - xh

    parts = {"b": (0, HALF), "b0": (0, QUARTER), "b1": (QUARTER, QUARTER)}
    parts.update({"a0": (HALF, QUARTER), "a1": (HALF + QUARTER, QUARTER)})
    b_down, b_up, b_far = down * 2 + xh, up * 2 + xh, far * 2 + xh
    o_down, o_up, o_far = down * 2 + 1 - xh, up * 2 + 1 - xh, far * 2 + 1 - xh
    moves = {
        "oub": (bo, "b", dev_up), "odb": (bo, "b", dev_down),
        "xa0": (bo, "a0", dev_x), "xa1": (bo, "a1", dev_x), "xob": (bo, "b", dev_x),
        "oua0": (bo, "a0", dev_up), "oda1": (bo, "a1", dev_down),
        "oua1": (bo, "a1", dev_up), "oda0": (bo, "a0", dev_down),
        "rbu": (b_down, "b0", dev_up), "rbd": (b_up, "b1", dev_down),
        "xdb": (b_down, "b", dev_x), "xub": (b_up, "b", dev_x),
        "pu0": (bp, "a0", dev_up), "pd1": (bp, "a1", dev_down),
        "pu1": (bp, "a1", dev_up), "pd0": (bp, "a0", dev_down),
        "rau": (b_down, "a0", dev_up), "rad": (b_up, "a1", dev_down),
        "xf0": (b_far, "b0", dev_x), "xf1": (b_far, "b1", dev_x),
        "rpu": (o_down, "a0", dev_up), "rpd": (o_up, "a1", dev_down),
    }
    order = list(moves)

    def b_copy(k):
        b, part, dev = moves[k]
        lo, n = parts[part]
        at = order.index(k)
        ref = g.at[b, pl.ds(lo, n)]
        return remote(ref, ref, b_ss.at[at], b_rs.at[at], dev)

    def b_start(names):
        for k in names.split():
            b_copy(k).start()

    def b_wait(names):
        for k in names.split():
            b_copy(k).wait_recv()

    def select(k, c):
        g[bo, pl.ds(pl.multiple_of(k * PIECE, PIECE), PIECE)] = ra[own_tab[0, k]]
        return c

    def project(part, *blocks):
        for b in blocks:
            out = dot(g[b, pl.ds(part * HALF, HALF)], w2[...]).astype(BF16)
            for u in range(2):
                kv[2 * part + u, pl.ds(pl.multiple_of(b * 32, 32), 32), :] = out[u * 32:(u + 1) * 32]

    each(a_copy, wait_recv)
    lax.fori_loop(0, SLOTS, select, 0)
    b_start("oub odb xa0 xa1")
    b_start("xob oua0 oda1")
    b_start("oua1 oda0")
    project(0, bo)
    project(1, bo)
    b_wait("oub")
    b_start("rbu xdb")
    b_wait("odb")
    b_start("rbd xub")
    b_wait("xa0")
    b_start("pu0")
    b_wait("xa1")
    b_start("pd1 pu1 pd0")
    b_wait("oua0")
    b_start("rau")
    b_wait("oda1")
    b_start("rad")
    project(0, b_down, b_up)
    b_wait("xob")
    project(0, bp)
    project(1, bp)
    b_wait("rbu")
    b_start("xf0")
    b_wait("rbd")
    b_start("xf1")
    b_wait("pu0")
    b_start("rpu")
    b_wait("pd1")
    b_start("rpd")
    b_wait("oua1 oda0")
    project(1, b_down, b_up)
    project(0, b_far)
    b_wait("xdb")
    project(0, o_down)
    b_wait("xub")
    project(0, o_up)
    each(a_copy, wait_send)
    shift(0, cs, cn).wait()
    shift(1, qs, qn).wait()
    keep = lax.broadcasted_iota(jnp.int32, (STRETCH, FEAT), 0) == 0
    more = s < SEQ - 1
    for buf, landing in ((qs, qn), (cs, cn)):
        mine = buf[192:256, :].astype(F32)
        theirs = jnp.where(more, landing[...].astype(F32), 0.0)
        buf[192:256, :] = jnp.where(keep, mine, theirs).astype(BF16)
    b_wait("pu1 pd0")
    project(1, o_down, o_up)

    scale = HD ** (-0.5)
    left = lax.broadcasted_iota(jnp.int32, (STRETCH, 2 * HD), 1) < HD

    def pair_rows(v):
        zero = jnp.zeros_like(v)
        return jnp.concatenate([jnp.where(left, v, zero), jnp.where(left, zero, v)], axis=0)

    def attend(u):
        rows = slice(u * STRETCH, u * STRETCH + STRETCH)
        for hp in range(2):
            lanes = slice(hp * 256, hp * 256 + 256)
            vlanes = slice(FEAT + hp * 256, FEAT + hp * 256 + 256)
            qb = pair_rows(qs[rows, lanes])
            db_ = pair_rows(cs[rows, lanes])
            kk = kv[u, :, lanes]
            vv = kv[u, :, vlanes]
            sc = dot_nt(kk, qb) * scale
            w = jnp.exp(sc - jnp.max(sc, axis=0, keepdims=True))
            p = w * (1.0 / jnp.sum(w, axis=0, keepdims=True))
            rounded = p.astype(BF16)
            prob[2 * u + hp] = rounded
            dp = dot_nt(vv, db_)
            centre = jnp.sum(p * dp, axis=0, keepdims=True)
            ds = (p * (dp - centre)).astype(BF16)
            kg = (dot(ds, qb) * scale).astype(BF16)
            vg = dot(rounded, db_).astype(BF16)
            at = slice((u % 2) * 32, (u % 2) * 32 + 32)
            for b in range(8):
                kgv[u // 2, b % 2, b // 2, at, lanes] = kg[b * 32:(b + 1) * 32]
                kgv[u // 2, b % 2, b // 2, at, vlanes] = vg[b * 32:(b + 1) * 32]

    o_back = remote(obuf.at[pl.ds(192, 64)], on, q_ss.at[2], q_rs.at[2], dev_next)

    def term(part, col):
        out = dot(kgv[part, col].reshape(4 * HALF, 2 * FEAT), w2t[...])
        terms[part, col] = out.reshape(4, HALF, WIDTH)

    oc = 1 - xh
    q0, q1 = pl.ds(0, QUARTER), pl.ds(QUARTER, QUARTER)
    both_q = pl.ds(0, HALF)
    c_moves = {}
    for k, name in enumerate(("xbf", "xbu", "xbd", "xbo")):
        c_moves[name] = (xb_s, xb_r, (k, both_q), dev_x)
    for h, name in enumerate("po"):
        c_moves["fu" + name] = (fa_s, fa_r, (h, q0), dev_up)
        c_moves["fd" + name] = (fa_s, fa_r, (h, q1), dev_down)
        c_moves["nu" + name] = (na_s, na_r, (h, 0, q1), dev_up)
        c_moves["nd" + name] = (na_s, na_r, (h, 1, q0), dev_down)
        c_moves["mu" + name] = (na_s, na_r, (h, 0, q0), dev_up)
        c_moves["md" + name] = (na_s, na_r, (h, 1, q1), dev_down)
    c_moves["fub"] = (fb_s, fb_r, (q0,), dev_up)
    c_moves["fdb"] = (fb_s, fb_r, (q1,), dev_down)
    c_moves["nub"] = (nb_s, nb_r, (0, q1), dev_up)
    c_moves["ndb"] = (nb_s, nb_r, (1, q0), dev_down)
    c_moves["mub"] = (nb_s, nb_r, (0, q0), dev_up)
    c_moves["mdb"] = (nb_s, nb_r, (1, q1), dev_down)
    c_moves["xs0"] = (xa_s, xa_r, (q0,), dev_x)
    c_moves["xs1"] = (xa_s, xa_r, (q1,), dev_x)
    c_order = list(c_moves)

    def c_copy(k):
        src, dst, part, dev = c_moves[k]
        at = c_order.index(k)
        return remote(src.at[part], dst.at[part], c_ss.at[at], c_rs.at[at], dev)

    def c_start(*names):
        for k in names:
            c_copy(k).start()

    def c_wait(*names):
        for k in names:
            c_copy(k).wait_recv()

    lo_q, hi_q = slice(0, QUARTER), slice(QUARTER, HALF)

    def far_out(h, col):
        fa_s[h] = terms[1, col, far].astype(BF16)

    def near_out(h, col):
        na_s[h, 0, hi_q] = terms[1, col, up, hi_q].astype(BF16)
        na_s[h, 1, lo_q] = terms[1, col, down, lo_q].astype(BF16)

    def merge_up(h, col):
        na_s[h, 0, lo_q] = (terms[1, col, up, lo_q] + fa_r[h, lo_q].astype(F32)).astype(BF16)

    def merge_down(h, col):
        na_s[h, 1, hi_q] = (terms[1, col, down, hi_q] + fa_r[h, hi_q].astype(F32)).astype(BF16)

    b_wait("xf0 xf1")
    project(0, o_far)
    attend(0)
    attend(1)
    term(0, oc)
    for k, at in enumerate((far, up, down, y)):
        xb_s[k] = terms[0, oc, at].astype(BF16)
    c_start("xbf", "xbu", "xbd", "xbo")
    b_wait("rau rad")
    project(1, b_far)
    b_wait("rpu rpd")
    project(1, o_far)
    attend(2)
    attend(3)
    term(1, oc)
    far_out(0, oc)
    c_start("fup", "fdp")
    near_out(0, oc)
    c_start("nup", "ndp")
    term(1, xh)
    far_out(1, xh)
    c_start("fuo", "fdo")
    term(0, xh)
    c_wait("xbf")
    fb_s[...] = (terms[0, xh, far] + xb_r[0].astype(F32)).astype(BF16)
    c_start("fub", "fdb")
    c_wait("fup")
    merge_up(0, oc)
    c_start("mup")
    c_wait("fdp")
    merge_down(0, oc)
    c_start("mdp")
    near_out(1, xh)
    c_start("nuo", "ndo")
    c_wait("xbu")
    v_up = terms[0, xh, up] + xb_r[1].astype(F32)
    terms[0, xh, up] = v_up
    nb_s[0, hi_q] = v_up[hi_q].astype(BF16)
    c_start("nub")
    c_wait("xbd")
    v_down = terms[0, xh, down] + xb_r[2].astype(F32)
    terms[0, xh, down] = v_down
    nb_s[1, lo_q] = v_down[lo_q].astype(BF16)
    c_start("ndb")
    c_wait("fuo")
    merge_up(1, xh)
    c_start("muo")
    c_wait("fdo")
    merge_down(1, xh)
    c_start("mdo")
    c_wait("fub")
    nb_s[0, lo_q] = (terms[0, xh, up, lo_q] + fb_r[lo_q].astype(F32)).astype(BF16)
    c_start("mub")
    c_wait("fdb")
    nb_s[1, hi_q] = (terms[0, xh, down, hi_q] + fb_r[hi_q].astype(F32)).astype(BF16)
    c_start("mdb")
    c_wait("nup", "ndp", "mup", "mdp")
    s_p = terms[1, oc, y] + na_r[0, 0].astype(F32) + na_r[0, 1].astype(F32)
    xa_s[...] = s_p.astype(BF16)
    c_start("xs0", "xs1")
    c_wait("xbo", "nub", "ndb", "mub", "mdb")
    s_b = terms[0, xh, y] + xb_r[3].astype(F32) + nb_r[0].astype(F32) + nb_r[1].astype(F32)
    fin[0:SLOTS // 2] = s_b.astype(BF16).reshape(SLOTS // 2, PIECE, WIDTH)
    c_wait("nuo", "ndo", "muo", "mdo")
    s_o = terms[1, xh, y] + na_r[1, 0].astype(F32) + na_r[1, 1].astype(F32)
    c_wait("xs0", "xs1")
    s_o = s_o + xa_r[...].astype(F32)
    fin[SLOTS // 2:] = s_o.astype(BF16).reshape(SLOTS // 2, PIECE, WIDTH)

    def give(j, c):
        q = (me + j) % GROUPS
        sd[2 * q] = fin[slot_tab[0, 2 * q]]
        sd[2 * q + 1] = fin[slot_tab[0, 2 * q + 1]]
        d_copy(j).start()
        return c

    lax.fori_loop(1, GROUPS, give, 0)
    rd[2 * me] = fin[slot_tab[0, 2 * me]]
    rd[2 * me + 1] = fin[slot_tab[0, 2 * me + 1]]

    for u in (3, 0, 1, 2):
        rows = slice(u * STRETCH, u * STRETCH + STRETCH)
        for hp in range(2):
            o = dot_tn(prob[2 * u + hp], kv[u, :, FEAT + hp * 256:FEAT + hp * 256 + 256])
            o = jnp.where(left, o[:STRETCH], o[STRETCH:])
            obuf[rows, hp * 256:hp * 256 + 256] = o.astype(BF16)
        if u == 3:
            o_back.start()
    for lo in range(0, FFN, 128):
        winT[lo:lo + 128, :] = win[:, lo:lo + 128].T
        woutT[:, lo:lo + 128] = wout[lo:lo + 128, :].T

    o_back.wait()
    edge = jnp.where(s > 0, on[...].astype(F32), 0.0)
    tail = jnp.where(keep, obuf[192:256, :].astype(F32), edge)
    whole = jnp.concatenate([obuf[0:192, :].astype(F32), tail], axis=0)
    att_out[...] = pltpu.roll(whole, STRETCH - 1, 0).astype(BF16)

    for k in order:
        b_copy(k).wait_send()
    for k in c_order:
        c_copy(k).wait_send()

    each(d_copy, wait_recv)
    rg = dot(onehot[...], rd[...].reshape(2 * GROUPS * PIECE, WIDTH))
    rgrad[...] = rg
    normed[...] = rg.astype(BF16)
    for lo in range(0, FFN, 256):
        d_act = dot(normed[...], woutT[:, lo:lo + 256])
        active[:, lo:lo + 256] = (d_act * gd[:, lo:lo + 256]).astype(BF16)
    mean = jnp.zeros((TOK, 1), F32)
    for lo, n in ((0, 512), (512, 384)):
        part = dot(active[...], winT[:, lo:lo + n]) * gain_row[:, lo:lo + n]
        dnorm[:, lo:lo + n] = part
        rows = db[:, :, lo:lo + n].reshape(TOK, n).astype(F32)
        mean = mean + jnp.sum(part * rows, axis=-1, keepdims=True)
    inv = inv_s[:, 0:1]
    xv = db[...].reshape(TOK, WIDTH).astype(F32)
    cubed = inv * inv * inv * (mean * (1.0 / WIDTH))
    out = rgrad[...] + inv * dnorm[...] - xv * cubed
    grad_out[...] = out.astype(BF16).reshape(ROWS, PIECE, WIDTH)
    each(d_copy, wait_send)


def body(hidden, w_query, w_key, w_value, enc_gain, w_in, w_out, db_states, neighbours, d_attended):
    hbm = pl.BlockSpec(memory_space=pl.ANY)
    vmem = pl.BlockSpec(memory_space=pltpu.VMEM)
    smem = pl.BlockSpec(memory_space=pltpu.SMEM)
    dma = pltpu.SemaphoreType.DMA
    vm = pltpu.VMEM
    scratch = [
        pltpu.SMEM((GROUPS, 128), jnp.int32),
        pltpu.SMEM((3, GROUPS), jnp.int32),
        pltpu.SMEM((1, SLOTS), jnp.int32),
        pltpu.SMEM((1, 2 * GROUPS), jnp.int32),
        vm((ROWS, PIECE, WIDTH), BF16),
        vm((WIDTH, FFN), BF16),
        vm((FFN, WIDTH), BF16),
        vm((FFN, WIDTH), BF16),
        vm((WIDTH, FFN), BF16),
        vm((WIDTH, 2 * FEAT), BF16),
        vm((2 * FEAT, WIDTH), BF16),
        vm((TOK, DM), BF16),
        vm((DM, FEAT), BF16),
        vm((TOK, FEAT), BF16),
        vm((TOK, WIDTH), BF16),
        vm((TOK, FFN), BF16),
        vm((TOK, FFN), F32),
        vm((TOK, 128), F32),
        vm((TOK, 512), BF16),
        vm((TOK, FEAT), F32),
        vm((TOK, FEAT), BF16),
        vm((TOK, FEAT), BF16),
        vm((STRETCH, FEAT), BF16),
        vm((STRETCH, FEAT), BF16),
        vm((TOK, FEAT), BF16),
        vm((STRETCH, FEAT), BF16),
        vm((ROWS, PIECE, WIDTH), BF16),
        vm((2 * GROUPS, PIECE, WIDTH), BF16),
        vm((2 * GROUPS, PIECE, WIDTH), BF16),
        vm((8, BLOCK, WIDTH), BF16),
        vm((4, 256, 2 * FEAT), BF16),
        vm((8, 256, 2 * STRETCH), BF16),
        vm((2, 2, 4, HALF, 2 * FEAT), BF16),
        vm((2, 2, 4, HALF, WIDTH), F32),
        vm((4, HALF, WIDTH), BF16), vm((4, HALF, WIDTH), BF16),
        vm((2, HALF, WIDTH), BF16), vm((2, HALF, WIDTH), BF16),
        vm((2, 2, HALF, WIDTH), BF16), vm((2, 2, HALF, WIDTH), BF16),
        vm((HALF, WIDTH), BF16), vm((HALF, WIDTH), BF16),
        vm((2, HALF, WIDTH), BF16), vm((2, HALF, WIDTH), BF16),
        vm((HALF, WIDTH), BF16), vm((HALF, WIDTH), BF16),
        vm((SLOTS, PIECE, WIDTH), BF16),
        vm((2 * GROUPS, PIECE, WIDTH), BF16),
        vm((2 * GROUPS, PIECE, WIDTH), BF16),
        vm((TOK, WIDTH), F32),
        vm((TOK, WIDTH), F32),
        dma((16,)),
        dma((16,)), dma((16,)),
        dma((16,)), dma((16,)),
        dma((16,)), dma((16,)),
        dma((24,)), dma((24,)),
        dma((24,)), dma((24,)),
        dma((3,)), dma((3,)),
    ]
    return pl.pallas_call(
        kernel,
        name="neighbour_attention",
        out_shape=(
            pltpu.VMEM((TOK, FEAT), BF16),
            pltpu.VMEM((ROWS, PIECE, WIDTH), BF16),
        ),
        in_specs=[smem, hbm, hbm, hbm, hbm, hbm, vmem, hbm, hbm, hbm],
        out_specs=(vmem, vmem),
        scratch_shapes=scratch,
        compiler_params=pltpu.CompilerParams(
            collective_id=0, has_side_effects=True, vmem_limit_bytes=56 * 1024 * 1024
        ),
    )(
        neighbours.T, db_states, hidden, w_query, w_key, w_value,
        enc_gain, w_in, w_out, d_attended,
    )


def solution(mesh):
    in_specs = (
        P(("role", "seq"), None),
        P(None, "tp"),
        P(None, "tp"),
        P(None, "tp"),
        P(),
        P(),
        P(),
        P(("role", "seq"), "tp", None),
        P(("role", "seq"), None),
        P(("role", "seq"), "tp"),
    )
    out_specs = (P(("role", "seq"), "tp"), P(("role", "seq"), "tp", None))
    return jax.shard_map(body, mesh=mesh, in_specs=in_specs, out_specs=out_specs, check_vma=False)
```

```python
import jax
import jax.numpy as jnp
from jax import lax
from jax.experimental import pallas as pl
from jax.experimental.pallas import tpu as pltpu
from jax.sharding import PartitionSpec as P

HD = 128
STRETCH = 64
EPS = 1e-06
MESH = pl.DeviceIdType.MESH
BF16 = jnp.bfloat16
F32 = jnp.float32
GELU_A = 0.7978845608028654
GELU_B = 0.044715

GROUPS = 16
SEQ = 8
ROWS = 16
SLOTS = 8
PIECE = 16
WIDTH = 896
FFN = 1792
TOK = 256
DM = 8192
FEAT = 512
BLOCK = SLOTS * PIECE
HALF = BLOCK // 2
QUARTER = BLOCK // 4
QK = 1024
QSTEPS = DM // QK


def dot(a, b):
    return jnp.dot(a, b, preferred_element_type=F32)


def dot_nt(a, b):
    return lax.dot_general(a, b, (((1,), (1,)), ((), ())), preferred_element_type=F32)


def dot_tn(a, b):
    return lax.dot_general(a, b, (((0,), (0,)), ((), ())), preferred_element_type=F32)


def kernel(
    nb, db_hbm, hid_hbm, wq_hbm, wk_hbm, wv_hbm, gain, win_hbm, wout_hbm, cot_hbm,
    att_out, grad_out,
    ids, row_tab, own_tab, slot_tab,
    db, win, wout, winT, woutT, w2, w2t, hid, wq, cot,
    normed, active, gd, inv_s, onehot, qacc, qs, cs, qn, cn, obuf, on,
    enc, sa, ra, g, kv, prob, kgv, terms,
    xb_s, xb_r, fa_s, fa_r, na_s, na_r, fb_s, fb_r, nb_s, nb_r, xa_s, xa_r,
    fin, sd, rd, rgrad, dnorm,
    lsem, ids_ss, ids_rs, a_ss, a_rs, d_ss, d_rs, b_ss, b_rs, c_ss, c_rs, q_ss, q_rs,
):
    r = lax.axis_index("role")
    s = lax.axis_index("seq")
    t = lax.axis_index("tp")
    y = t // 2
    xh = t % 2
    me = r * SEQ + s
    up = (y + 1) % 4
    down = (y + 3) % 4
    far = (y + 2) % 4
    dev_up = (r, s, up * 2 + xh)
    dev_down = (r, s, down * 2 + xh)
    dev_x = (r, s, y * 2 + 1 - xh)
    dev_next = (r, (s + 1) % SEQ, t)
    dev_prev = (r, (s + SEQ - 1) % SEQ, t)

    def remote(src, dst, ss, rs, dev):
        return pltpu.make_async_remote_copy(
            src_ref=src, dst_ref=dst, send_sem=ss, recv_sem=rs, device_id=dev, device_id_type=MESH
        )

    loads = []

    def load(src, dst):
        cp = pltpu.make_async_copy(src, dst, lsem.at[len(loads)])
        cp.start()
        loads.append(cp)
        return cp

    l_db = load(db_hbm, db)
    l_win = load(win_hbm, win)

    barrier = pltpu.get_barrier_semaphore()

    def greet(dev):
        pl.semaphore_signal(barrier, inc=1, device_id=dev, device_id_type=MESH)

    def peer(j):
        q = (me + j) % GROUPS
        return q, (q // SEQ, q % SEQ, t)

    def greet_group(j, c):
        greet(peer(j)[1])
        return c

    lax.fori_loop(1, GROUPS, greet_group, 0)
    greet(dev_up)
    greet(dev_down)
    greet(dev_x)

    def copy_ids(i, c):
        ids[me, i] = nb[i % 2, i // 2]
        return c

    lax.fori_loop(0, SLOTS, copy_ids, 0)

    pl.semaphore_wait(barrier, 18)

    def each(make, act):
        def step(j, c):
            act(make(j))
            return c

        lax.fori_loop(1, GROUPS, step, 0)

    def ids_copy(j):
        return remote(ids.at[me], ids.at[me], ids_ss.at[j], ids_rs.at[j], peer(j)[1])

    start = lambda cp: cp.start()
    wait_recv = lambda cp: cp.wait_recv()
    wait_send = lambda cp: cp.wait_send()

    each(ids_copy, start)

    l_db.wait()
    xv = db[...].reshape(TOK, WIDTH).astype(F32)
    inverse = lax.rsqrt(jnp.mean(xv * xv, axis=-1, keepdims=True) + EPS)
    inv_s[...] = jnp.broadcast_to(inverse, (TOK, 128))
    gain_row = gain[...].reshape(1, WIDTH)
    normed[...] = (xv * inverse * gain_row).astype(BF16)
    l_win.wait()
    l_wout = load(wout_hbm, wout)

    for lo in range(0, FFN, 256):
        cols = slice(lo, lo + 256)
        pre = dot(normed[...], win[:, cols])
        gd[:, cols] = pre
        th = jnp.tanh(GELU_A * (pre + GELU_B * (pre * pre * pre)))
        active[:, cols] = (pre * (0.5 * (1.0 + th))).astype(BF16)
    l_wout.wait()

    l_cot = load(cot_hbm, cot)
    l_hid = load(hid_hbm, hid)
    l_wq = [
        load(wq_hbm.at[pl.ds(i * QK, QK)], wq.at[pl.ds(i * QK, QK)]) for i in range(QSTEPS)
    ]
    l_wk = load(wk_hbm, w2.at[:, pl.ds(0, FEAT)])
    l_wv = load(wv_hbm, w2.at[:, pl.ds(FEAT, FEAT)])

    rows = db[...].reshape(TOK, WIDTH).astype(F32)
    coded = rows + dot(active[...], wout[...])
    enc[...] = coded.astype(BF16).reshape(ROWS, PIECE, WIDTH)

    def row_step(q):
        cnt = jnp.int32(0)
        row0 = jnp.int32(0)
        row1 = jnp.int32(0)
        for k in range(SLOTS):
            v = ids[q, k] - me * ROWS
            hit = (v >= 0) & (v < ROWS)
            row0 = jnp.where(hit & (cnt == 0), v, row0)
            row1 = jnp.where(hit & (cnt == 1), v, row1)
            cnt = cnt + hit.astype(jnp.int32)
        row_tab[0, q] = row0
        row_tab[1, q] = row1
        row_tab[2, q] = cnt
        return row0, row1

    def exchange(src, dst, ss, rs):
        def make(j):
            q, dev = peer(j)
            return remote(src.at[pl.ds(2 * q, 2)], dst.at[pl.ds(2 * me, 2)], ss.at[j], rs.at[j], dev)

        return make

    a_copy = exchange(sa, ra, a_ss, a_rs)
    d_copy = exchange(sd, rd, d_ss, d_rs)

    def serve(j, c):
        ids_copy(GROUPS - j).wait_recv()
        q = (me + j) % GROUPS
        row0, row1 = row_step(q)
        sa[2 * q] = enc[row0]
        sa[2 * q + 1] = enc[row1]
        a_copy(j).start()
        return c

    lax.fori_loop(1, GROUPS, serve, 0)
    row0, row1 = row_step(me)
    ra[2 * me] = enc[row0]
    ra[2 * me + 1] = enc[row1]

    def own_step(k, c):
        v = ids[me, k]
        owner = v // ROWS
        rank = jnp.int32(0)
        for e in range(SLOTS):
            same = (ids[me, e] // ROWS == owner) & (e < k)
            rank = rank + same.astype(jnp.int32)
        own_tab[0, k] = owner * 2 + rank
        return c

    lax.fori_loop(0, SLOTS, own_step, 0)

    def slot_step(q, c):
        slot = jnp.int32(0)
        for k in range(SLOTS):
            slot = jnp.where(own_tab[0, k] == q, k, slot)
        slot_tab[0, q] = slot
        return c

    lax.fori_loop(0, 2 * GROUPS, slot_step, 0)

    def shift(k, buf, landing):
        return remote(buf.at[pl.ds(192, 64)], landing, q_ss.at[k], q_rs.at[k], dev_prev)

    l_cot.wait()
    cs[...] = pltpu.roll(cot[...].astype(F32), TOK - (STRETCH - 1), 0).astype(BF16)
    shift(0, cs, cn).start()
    l_hid.wait()

    def query_step(i):
        l_wq[i].wait()
        part = dot(hid[:, i * QK:(i + 1) * QK], wq[pl.ds(i * QK, QK), :])
        if i == 0:
            qacc[...] = part
        else:
            qacc[...] += part

    def query_end():
        turned = pltpu.roll(qacc[...].astype(BF16).astype(F32), TOK - (STRETCH - 1), 0)
        qs[...] = turned.astype(BF16)
        shift(1, qs, qn).start()

    def build_selection():
        lane_k = lax.broadcasted_iota(jnp.int32, (8, 512), 1) // PIECE

        def col_step(q, cols):
            cnt = row_tab[2, q]
            first = jnp.where(cnt > 0, row_tab[0, q], -1)
            second = jnp.where(cnt > 1, row_tab[1, q], -1)
            cols = jnp.where(lane_k == 2 * q, first, cols)
            return jnp.where(lane_k == 2 * q + 1, second, cols)

        cols = lax.fori_loop(0, GROUPS, col_step, jnp.full((8, 512), -1, jnp.int32))
        row_i = lax.broadcasted_iota(jnp.int32, (TOK, 512), 0)
        col_i = lax.broadcasted_iota(jnp.int32, (TOK, 512), 1)
        match = (row_i // PIECE == cols[0:1, :]) & (row_i % PIECE == col_i % PIECE)
        onehot[...] = jnp.where(match, 1.0, 0.0).astype(BF16)

    def derive(c, carry):
        cols = pl.ds(pl.multiple_of(c * 256, 256), 256)
        pre = gd[:, cols]
        sq = pre * pre
        th = jnp.tanh(GELU_A * (pre + GELU_B * (sq * pre)))
        slope = pre * (0.5 * GELU_A) * (1.0 - th * th) * (1.0 + 3.0 * GELU_B * sq)
        gd[:, cols] = 0.5 * (1.0 + th) + slope
        return carry

    lax.fori_loop(0, FFN // 256, derive, 0)
    for i in range(QSTEPS):
        query_step(i)
    query_end()
    l_wk.wait()
    l_wv.wait()
    for lo in range(0, WIDTH, 128):
        w2t[:, lo:lo + 128] = w2[lo:lo + 128, :].T
    build_selection()
    each(ids_copy, wait_send)

    bo = t
    bp = y * 2 + 1 - xh

    parts = {"b": (0, HALF), "b0": (0, QUARTER), "b1": (QUARTER, QUARTER)}
    parts.update({"a0": (HALF, QUARTER), "a1": (HALF + QUARTER, QUARTER)})
    b_down, b_up, b_far = down * 2 + xh, up * 2 + xh, far * 2 + xh
    o_down, o_up, o_far = down * 2 + 1 - xh, up * 2 + 1 - xh, far * 2 + 1 - xh
    moves = {
        "oub": (bo, "b", dev_up), "odb": (bo, "b", dev_down),
        "xa0": (bo, "a0", dev_x), "xa1": (bo, "a1", dev_x), "xob": (bo, "b", dev_x),
        "oua0": (bo, "a0", dev_up), "oda1": (bo, "a1", dev_down),
        "oua1": (bo, "a1", dev_up), "oda0": (bo, "a0", dev_down),
        "rbu": (b_down, "b0", dev_up), "rbd": (b_up, "b1", dev_down),
        "xdb": (b_down, "b", dev_x), "xub": (b_up, "b", dev_x),
        "pu0": (bp, "a0", dev_up), "pd1": (bp, "a1", dev_down),
        "pu1": (bp, "a1", dev_up), "pd0": (bp, "a0", dev_down),
        "rau": (b_down, "a0", dev_up), "rad": (b_up, "a1", dev_down),
        "xf0": (b_far, "b0", dev_x), "xf1": (b_far, "b1", dev_x),
        "rpu": (o_down, "a0", dev_up), "rpd": (o_up, "a1", dev_down),
    }
    order = list(moves)

    def b_copy(k):
        b, part, dev = moves[k]
        lo, n = parts[part]
        at = order.index(k)
        ref = g.at[b, pl.ds(lo, n)]
        return remote(ref, ref, b_ss.at[at], b_rs.at[at], dev)

    def b_start(names):
        for k in names.split():
            b_copy(k).start()

    def b_wait(names):
        for k in names.split():
            b_copy(k).wait_recv()

    def select(k, c):
        g[bo, pl.ds(pl.multiple_of(k * PIECE, PIECE), PIECE)] = ra[own_tab[0, k]]
        return c

    def project(part, *blocks):
        for b in blocks:
            out = dot(g[b, pl.ds(part * HALF, HALF)], w2[...]).astype(BF16)
            for u in range(2):
                kv[2 * part + u, pl.ds(pl.multiple_of(b * 32, 32), 32), :] = out[u * 32:(u + 1) * 32]

    each(a_copy, wait_recv)
    lax.fori_loop(0, SLOTS, select, 0)
    b_start("oub odb xa0 xa1")
    b_start("xob oua0 oda1")
    b_start("oua1 oda0")
    project(0, bo)
    project(1, bo)
    b_wait("oub")
    b_start("rbu xdb")
    b_wait("odb")
    b_start("rbd xub")
    b_wait("xa0")
    b_start("pu0")
    b_wait("xa1")
    b_start("pd1 pu1 pd0")
    b_wait("oua0")
    b_start("rau")
    b_wait("oda1")
    b_start("rad")
    project(0, b_down, b_up)
    b_wait("xob")
    project(0, bp)
    project(1, bp)
    b_wait("rbu")
    b_start("xf0")
    b_wait("rbd")
    b_start("xf1")
    b_wait("pu0")
    b_start("rpu")
    b_wait("pd1")
    b_start("rpd")
    b_wait("oua1 oda0")
    project(1, b_down, b_up)
    project(0, b_far)
    b_wait("xdb")
    project(0, o_down)
    b_wait("xub")
    project(0, o_up)
    each(a_copy, wait_send)
    shift(0, cs, cn).wait()
    shift(1, qs, qn).wait()
    keep = lax.broadcasted_iota(jnp.int32, (STRETCH, FEAT), 0) == 0
    more = s < SEQ - 1
    for buf, landing in ((qs, qn), (cs, cn)):
        mine = buf[192:256, :].astype(F32)
        theirs = jnp.where(more, landing[...].astype(F32), 0.0)
        buf[192:256, :] = jnp.where(keep, mine, theirs).astype(BF16)
    b_wait("pu1 pd0")
    project(1, o_down, o_up)

    scale = HD ** (-0.5)
    left = lax.broadcasted_iota(jnp.int32, (STRETCH, 2 * HD), 1) < HD

    def pair_rows(v):
        zero = jnp.zeros_like(v)
        return jnp.concatenate([jnp.where(left, v, zero), jnp.where(left, zero, v)], axis=0)

    def attend(u):
        rows = slice(u * STRETCH, u * STRETCH + STRETCH)
        for hp in range(2):
            lanes = slice(hp * 256, hp * 256 + 256)
            vlanes = slice(FEAT + hp * 256, FEAT + hp * 256 + 256)
            qb = pair_rows(qs[rows, lanes])
            db_ = pair_rows(cs[rows, lanes])
            kk = kv[u, :, lanes]
            vv = kv[u, :, vlanes]
            sc = dot_nt(kk, qb) * scale
            w = jnp.exp(sc - jnp.max(sc, axis=0, keepdims=True))
            p = w * (1.0 / jnp.sum(w, axis=0, keepdims=True))
            rounded = p.astype(BF16)
            prob[2 * u + hp] = rounded
            dp = dot_nt(vv, db_)
            centre = jnp.sum(p * dp, axis=0, keepdims=True)
            ds = (p * (dp - centre)).astype(BF16)
            kg = (dot(ds, qb) * scale).astype(BF16)
            vg = dot(rounded, db_).astype(BF16)
            at = slice((u % 2) * 32, (u % 2) * 32 + 32)
            for b in range(8):
                kgv[u // 2, b % 2, b // 2, at, lanes] = kg[b * 32:(b + 1) * 32]
                kgv[u // 2, b % 2, b // 2, at, vlanes] = vg[b * 32:(b + 1) * 32]

    o_back = remote(obuf.at[pl.ds(192, 64)], on, q_ss.at[2], q_rs.at[2], dev_next)

    def term(part, col):
        out = dot(kgv[part, col].reshape(4 * HALF, 2 * FEAT), w2t[...])
        terms[part, col] = out.reshape(4, HALF, WIDTH)

    oc = 1 - xh
    q0, q1 = pl.ds(0, QUARTER), pl.ds(QUARTER, QUARTER)
    both_q = pl.ds(0, HALF)
    c_moves = {}
    for k, name in enumerate(("xbf", "xbu", "xbd", "xbo")):
        c_moves[name] = (xb_s, xb_r, (k, both_q), dev_x)
    for h, name in enumerate("po"):
        c_moves["fu" + name] = (fa_s, fa_r, (h, q0), dev_up)
        c_moves["fd" + name] = (fa_s, fa_r, (h, q1), dev_down)
        c_moves["nu" + name] = (na_s, na_r, (h, 0, q1), dev_up)
        c_moves["nd" + name] = (na_s, na_r, (h, 1, q0), dev_down)
        c_moves["mu" + name] = (na_s, na_r, (h, 0, q0), dev_up)
        c_moves["md" + name] = (na_s, na_r, (h, 1, q1), dev_down)
    c_moves["fub"] = (fb_s, fb_r, (q0,), dev_up)
    c_moves["fdb"] = (fb_s, fb_r, (q1,), dev_down)
    c_moves["nub"] = (nb_s, nb_r, (0, q1), dev_up)
    c_moves["ndb"] = (nb_s, nb_r, (1, q0), dev_down)
    c_moves["mub"] = (nb_s, nb_r, (0, q0), dev_up)
    c_moves["mdb"] = (nb_s, nb_r, (1, q1), dev_down)
    c_moves["xs0"] = (xa_s, xa_r, (q0,), dev_x)
    c_moves["xs1"] = (xa_s, xa_r, (q1,), dev_x)
    c_order = list(c_moves)

    def c_copy(k):
        src, dst, part, dev = c_moves[k]
        at = c_order.index(k)
        return remote(src.at[part], dst.at[part], c_ss.at[at], c_rs.at[at], dev)

    def c_start(*names):
        for k in names:
            c_copy(k).start()

    def c_wait(*names):
        for k in names:
            c_copy(k).wait_recv()

    lo_q, hi_q = slice(0, QUARTER), slice(QUARTER, HALF)

    def far_out(h, col):
        fa_s[h] = terms[1, col, far].astype(BF16)

    def near_out(h, col):
        na_s[h, 0, hi_q] = terms[1, col, up, hi_q].astype(BF16)
        na_s[h, 1, lo_q] = terms[1, col, down, lo_q].astype(BF16)

    def merge_up(h, col):
        na_s[h, 0, lo_q] = (terms[1, col, up, lo_q] + fa_r[h, lo_q].astype(F32)).astype(BF16)

    def merge_down(h, col):
        na_s[h, 1, hi_q] = (terms[1, col, down, hi_q] + fa_r[h, hi_q].astype(F32)).astype(BF16)

    b_wait("rau rad")
    project(1, b_far)
    b_wait("rpu rpd")
    project(1, o_far)
    attend(2)
    attend(3)
    term(1, oc)
    far_out(0, oc)
    c_start("fup", "fdp")
    near_out(0, oc)
    c_start("nup", "ndp")
    b_wait("xf0 xf1")
    project(0, o_far)
    attend(0)
    attend(1)
    term(0, oc)
    for k, at in enumerate((far, up, down, y)):
        xb_s[k] = terms[0, oc, at].astype(BF16)
    c_start("xbf", "xbu", "xbd", "xbo")
    term(1, xh)
    far_out(1, xh)
    c_start("fuo", "fdo")
    term(0, xh)
    c_wait("xbf")
    fb_s[...] = (terms[0, xh, far] + xb_r[0].astype(F32)).astype(BF16)
    c_start("fub", "fdb")
    c_wait("fup")
    merge_up(0, oc)
    c_start("mup")
    c_wait("fdp")
    merge_down(0, oc)
    c_start("mdp")
    near_out(1, xh)
    c_start("nuo", "ndo")
    c_wait("xbu")
    v_up = terms[0, xh, up] + xb_r[1].astype(F32)
    terms[0, xh, up] = v_up
    nb_s[0, hi_q] = v_up[hi_q].astype(BF16)
    c_start("nub")
    c_wait("xbd")
    v_down = terms[0, xh, down] + xb_r[2].astype(F32)
    terms[0, xh, down] = v_down
    nb_s[1, lo_q] = v_down[lo_q].astype(BF16)
    c_start("ndb")
    c_wait("fuo")
    merge_up(1, xh)
    c_start("muo")
    c_wait("fdo")
    merge_down(1, xh)
    c_start("mdo")
    c_wait("fub")
    nb_s[0, lo_q] = (terms[0, xh, up, lo_q] + fb_r[lo_q].astype(F32)).astype(BF16)
    c_start("mub")
    c_wait("fdb")
    nb_s[1, hi_q] = (terms[0, xh, down, hi_q] + fb_r[hi_q].astype(F32)).astype(BF16)
    c_start("mdb")
    c_wait("nup", "ndp", "mup", "mdp")
    s_p = terms[1, oc, y] + na_r[0, 0].astype(F32) + na_r[0, 1].astype(F32)
    xa_s[...] = s_p.astype(BF16)
    c_start("xs0", "xs1")
    c_wait("xbo", "nub", "ndb", "mub", "mdb")
    s_b = terms[0, xh, y] + xb_r[3].astype(F32) + nb_r[0].astype(F32) + nb_r[1].astype(F32)
    fin[0:SLOTS // 2] = s_b.astype(BF16).reshape(SLOTS // 2, PIECE, WIDTH)
    c_wait("nuo", "ndo", "muo", "mdo")
    s_o = terms[1, xh, y] + na_r[1, 0].astype(F32) + na_r[1, 1].astype(F32)
    c_wait("xs0", "xs1")
    s_o = s_o + xa_r[...].astype(F32)
    fin[SLOTS // 2:] = s_o.astype(BF16).reshape(SLOTS // 2, PIECE, WIDTH)

    def give(j, c):
        q = (me + j) % GROUPS
        sd[2 * q] = fin[slot_tab[0, 2 * q]]
        sd[2 * q + 1] = fin[slot_tab[0, 2 * q + 1]]
        d_copy(j).start()
        return c

    lax.fori_loop(1, GROUPS, give, 0)
    rd[2 * me] = fin[slot_tab[0, 2 * me]]
    rd[2 * me + 1] = fin[slot_tab[0, 2 * me + 1]]

    for u in (3, 0, 1, 2):
        rows = slice(u * STRETCH, u * STRETCH + STRETCH)
        for hp in range(2):
            o = dot_tn(prob[2 * u + hp], kv[u, :, FEAT + hp * 256:FEAT + hp * 256 + 256])
            o = jnp.where(left, o[:STRETCH], o[STRETCH:])
            obuf[rows, hp * 256:hp * 256 + 256] = o.astype(BF16)
        if u == 3:
            o_back.start()
    for lo in range(0, FFN, 128):
        winT[lo:lo + 128, :] = win[:, lo:lo + 128].T
        woutT[:, lo:lo + 128] = wout[lo:lo + 128, :].T

    o_back.wait()
    edge = jnp.where(s > 0, on[...].astype(F32), 0.0)
    tail = jnp.where(keep, obuf[192:256, :].astype(F32), edge)
    whole = jnp.concatenate([obuf[0:192, :].astype(F32), tail], axis=0)
    att_out[...] = pltpu.roll(whole, STRETCH - 1, 0).astype(BF16)

    for k in order:
        b_copy(k).wait_send()
    for k in c_order:
        c_copy(k).wait_send()

    each(d_copy, wait_recv)
    rg = dot(onehot[...], rd[...].reshape(2 * GROUPS * PIECE, WIDTH))
    rgrad[...] = rg
    normed[...] = rg.astype(BF16)
    for lo in range(0, FFN, 256):
        d_act = dot(normed[...], woutT[:, lo:lo + 256])
        active[:, lo:lo + 256] = (d_act * gd[:, lo:lo + 256]).astype(BF16)
    mean = jnp.zeros((TOK, 1), F32)
    for lo, n in ((0, 512), (512, 384)):
        part = dot(active[...], winT[:, lo:lo + n]) * gain_row[:, lo:lo + n]
        dnorm[:, lo:lo + n] = part
        rows = db[:, :, lo:lo + n].reshape(TOK, n).astype(F32)
        mean = mean + jnp.sum(part * rows, axis=-1, keepdims=True)
    inv = inv_s[:, 0:1]
    xv = db[...].reshape(TOK, WIDTH).astype(F32)
    cubed = inv * inv * inv * (mean * (1.0 / WIDTH))
    out = rgrad[...] + inv * dnorm[...] - xv * cubed
    grad_out[...] = out.astype(BF16).reshape(ROWS, PIECE, WIDTH)
    each(d_copy, wait_send)


def body(hidden, w_query, w_key, w_value, enc_gain, w_in, w_out, db_states, neighbours, d_attended):
    hbm = pl.BlockSpec(memory_space=pl.ANY)
    vmem = pl.BlockSpec(memory_space=pltpu.VMEM)
    smem = pl.BlockSpec(memory_space=pltpu.SMEM)
    dma = pltpu.SemaphoreType.DMA
    vm = pltpu.VMEM
    scratch = [
        pltpu.SMEM((GROUPS, 128), jnp.int32),
        pltpu.SMEM((3, GROUPS), jnp.int32),
        pltpu.SMEM((1, SLOTS), jnp.int32),
        pltpu.SMEM((1, 2 * GROUPS), jnp.int32),
        vm((ROWS, PIECE, WIDTH), BF16),
        vm((WIDTH, FFN), BF16),
        vm((FFN, WIDTH), BF16),
        vm((FFN, WIDTH), BF16),
        vm((WIDTH, FFN), BF16),
        vm((WIDTH, 2 * FEAT), BF16),
        vm((2 * FEAT, WIDTH), BF16),
        vm((TOK, DM), BF16),
        vm((DM, FEAT), BF16),
        vm((TOK, FEAT), BF16),
        vm((TOK, WIDTH), BF16),
        vm((TOK, FFN), BF16),
        vm((TOK, FFN), F32),
        vm((TOK, 128), F32),
        vm((TOK, 512), BF16),
        vm((TOK, FEAT), F32),
        vm((TOK, FEAT), BF16),
        vm((TOK, FEAT), BF16),
        vm((STRETCH, FEAT), BF16),
        vm((STRETCH, FEAT), BF16),
        vm((TOK, FEAT), BF16),
        vm((STRETCH, FEAT), BF16),
        vm((ROWS, PIECE, WIDTH), BF16),
        vm((2 * GROUPS, PIECE, WIDTH), BF16),
        vm((2 * GROUPS, PIECE, WIDTH), BF16),
        vm((8, BLOCK, WIDTH), BF16),
        vm((4, 256, 2 * FEAT), BF16),
        vm((8, 256, 2 * STRETCH), BF16),
        vm((2, 2, 4, HALF, 2 * FEAT), BF16),
        vm((2, 2, 4, HALF, WIDTH), F32),
        vm((4, HALF, WIDTH), BF16), vm((4, HALF, WIDTH), BF16),
        vm((2, HALF, WIDTH), BF16), vm((2, HALF, WIDTH), BF16),
        vm((2, 2, HALF, WIDTH), BF16), vm((2, 2, HALF, WIDTH), BF16),
        vm((HALF, WIDTH), BF16), vm((HALF, WIDTH), BF16),
        vm((2, HALF, WIDTH), BF16), vm((2, HALF, WIDTH), BF16),
        vm((HALF, WIDTH), BF16), vm((HALF, WIDTH), BF16),
        vm((SLOTS, PIECE, WIDTH), BF16),
        vm((2 * GROUPS, PIECE, WIDTH), BF16),
        vm((2 * GROUPS, PIECE, WIDTH), BF16),
        vm((TOK, WIDTH), F32),
        vm((TOK, WIDTH), F32),
        dma((16,)),
        dma((16,)), dma((16,)),
        dma((16,)), dma((16,)),
        dma((16,)), dma((16,)),
        dma((24,)), dma((24,)),
        dma((24,)), dma((24,)),
        dma((3,)), dma((3,)),
    ]
    return pl.pallas_call(
        kernel,
        name="neighbour_attention",
        out_shape=(
            pltpu.VMEM((TOK, FEAT), BF16),
            pltpu.VMEM((ROWS, PIECE, WIDTH), BF16),
        ),
        in_specs=[smem, hbm, hbm, hbm, hbm, hbm, vmem, hbm, hbm, hbm],
        out_specs=(vmem, vmem),
        scratch_shapes=scratch,
        compiler_params=pltpu.CompilerParams(
            collective_id=0, has_side_effects=True, vmem_limit_bytes=56 * 1024 * 1024
        ),
    )(
        neighbours.T, db_states, hidden, w_query, w_key, w_value,
        enc_gain, w_in, w_out, d_attended,
    )


def solution(mesh):
    in_specs = (
        P(("role", "seq"), None),
        P(None, "tp"),
        P(None, "tp"),
        P(None, "tp"),
        P(),
        P(),
        P(),
        P(("role", "seq"), "tp", None),
        P(("role", "seq"), None),
        P(("role", "seq"), "tp"),
    )
    out_specs = (P(("role", "seq"), "tp"), P(("role", "seq"), "tp", None))
    return jax.shard_map(body, mesh=mesh, in_specs=in_specs, out_specs=out_specs, check_vma=False)
```

```python
import jax
import jax.numpy as jnp
from jax import lax
from jax.experimental import pallas as pl
from jax.experimental.pallas import tpu as pltpu
from jax.sharding import PartitionSpec as P

HD = 128
STRETCH = 64
EPS = 1e-06
MESH = pl.DeviceIdType.MESH
BF16 = jnp.bfloat16
F32 = jnp.float32
GELU_A = 0.7978845608028654
GELU_B = 0.044715

GROUPS = 16
SEQ = 8
ROWS = 16
SLOTS = 8
PIECE = 16
WIDTH = 896
FFN = 1792
TOK = 256
DM = 8192
FEAT = 512
BLOCK = SLOTS * PIECE
HALF = BLOCK // 2
QUARTER = BLOCK // 4
QK = 1024
QSTEPS = DM // QK


def dot(a, b):
    return jnp.dot(a, b, preferred_element_type=F32)


def dot_nt(a, b):
    return lax.dot_general(a, b, (((1,), (1,)), ((), ())), preferred_element_type=F32)


def dot_tn(a, b):
    return lax.dot_general(a, b, (((0,), (0,)), ((), ())), preferred_element_type=F32)


def kernel(
    nb, db_hbm, hid_hbm, wq_hbm, wk_hbm, wv_hbm, gain, win_hbm, wout_hbm, cot_hbm,
    att_out, grad_out,
    ids, row_tab, own_tab, slot_tab,
    db, win, wout, winT, woutT, w2, w2t, hid, wq, cot,
    normed, active, gd, inv_s, onehot, qacc, qs, cs, qn, cn, obuf, on,
    enc, sa, ra, g, kv, prob, kgv, terms,
    xb_s, xb_r, fa_s, fa_r, na_s, na_r, fb_s, fb_r, nb_s, nb_r, xa_s, xa_r,
    fin, sd, rd, rgrad, dnorm,
    lsem, ids_ss, ids_rs, a_ss, a_rs, d_ss, d_rs, b_ss, b_rs, c_ss, c_rs, q_ss, q_rs,
):
    r = lax.axis_index("role")
    s = lax.axis_index("seq")
    t = lax.axis_index("tp")
    y = t // 2
    xh = t % 2
    me = r * SEQ + s
    up = (y + 1) % 4
    down = (y + 3) % 4
    far = (y + 2) % 4
    dev_up = (r, s, up * 2 + xh)
    dev_down = (r, s, down * 2 + xh)
    dev_x = (r, s, y * 2 + 1 - xh)
    dev_next = (r, (s + 1) % SEQ, t)
    dev_prev = (r, (s + SEQ - 1) % SEQ, t)

    def remote(src, dst, ss, rs, dev):
        return pltpu.make_async_remote_copy(
            src_ref=src, dst_ref=dst, send_sem=ss, recv_sem=rs, device_id=dev, device_id_type=MESH
        )

    loads = []

    def load(src, dst):
        cp = pltpu.make_async_copy(src, dst, lsem.at[len(loads)])
        cp.start()
        loads.append(cp)
        return cp

    l_db = load(db_hbm, db)
    l_win = load(win_hbm, win)

    barrier = pltpu.get_barrier_semaphore()

    def greet(dev):
        pl.semaphore_signal(barrier, inc=1, device_id=dev, device_id_type=MESH)

    def peer(j):
        q = (me + j) % GROUPS
        return q, (q // SEQ, q % SEQ, t)

    def greet_group(j, c):
        greet(peer(j)[1])
        return c

    lax.fori_loop(1, GROUPS, greet_group, 0)
    greet(dev_up)
    greet(dev_down)
    greet(dev_x)

    def copy_ids(i, c):
        ids[me, i] = nb[i % 2, i // 2]
        return c

    lax.fori_loop(0, SLOTS, copy_ids, 0)

    pl.semaphore_wait(barrier, 18)

    def each(make, act):
        def step(j, c):
            act(make(j))
            return c

        lax.fori_loop(1, GROUPS, step, 0)

    def ids_copy(j):
        return remote(ids.at[me], ids.at[me], ids_ss.at[j], ids_rs.at[j], peer(j)[1])

    start = lambda cp: cp.start()
    wait_recv = lambda cp: cp.wait_recv()
    wait_send = lambda cp: cp.wait_send()

    each(ids_copy, start)

    l_db.wait()
    xv = db[...].reshape(TOK, WIDTH).astype(F32)
    inverse = lax.rsqrt(jnp.mean(xv * xv, axis=-1, keepdims=True) + EPS)
    inv_s[...] = jnp.broadcast_to(inverse, (TOK, 128))
    gain_row = gain[...].reshape(1, WIDTH)
    normed[...] = (xv * inverse * gain_row).astype(BF16)
    l_win.wait()
    l_wout = load(wout_hbm, wout)

    for lo in range(0, FFN, 256):
        cols = slice(lo, lo + 256)
        pre = dot(normed[...], win[:, cols])
        gd[:, cols] = pre
        th = jnp.tanh(GELU_A * (pre + GELU_B * (pre * pre * pre)))
        active[:, cols] = (pre * (0.5 * (1.0 + th))).astype(BF16)
    l_wout.wait()

    l_cot = load(cot_hbm, cot)
    l_hid = load(hid_hbm, hid)
    l_wq = [
        load(wq_hbm.at[pl.ds(i * QK, QK)], wq.at[pl.ds(i * QK, QK)]) for i in range(QSTEPS)
    ]
    l_wk = load(wk_hbm, w2.at[:, pl.ds(0, FEAT)])
    l_wv = load(wv_hbm, w2.at[:, pl.ds(FEAT, FEAT)])

    rows = db[...].reshape(TOK, WIDTH).astype(F32)
    coded = rows + dot(active[...], wout[...])
    enc[...] = coded.astype(BF16).reshape(ROWS, PIECE, WIDTH)

    def row_step(q):
        cnt = jnp.int32(0)
        row0 = jnp.int32(0)
        row1 = jnp.int32(0)
        for k in range(SLOTS):
            v = ids[q, k] - me * ROWS
            hit = (v >= 0) & (v < ROWS)
            row0 = jnp.where(hit & (cnt == 0), v, row0)
            row1 = jnp.where(hit & (cnt == 1), v, row1)
            cnt = cnt + hit.astype(jnp.int32)
        row_tab[0, q] = row0
        row_tab[1, q] = row1
        row_tab[2, q] = cnt
        return row0, row1

    def exchange(src, dst, ss, rs):
        def make(j):
            q, dev = peer(j)
            return remote(src.at[pl.ds(2 * q, 2)], dst.at[pl.ds(2 * me, 2)], ss.at[j], rs.at[j], dev)

        return make

    a_copy = exchange(sa, ra, a_ss, a_rs)
    d_copy = exchange(sd, rd, d_ss, d_rs)

    def serve(j, c):
        ids_copy(GROUPS - j).wait_recv()
        q = (me + j) % GROUPS
        row0, row1 = row_step(q)
        sa[2 * q] = enc[row0]
        sa[2 * q + 1] = enc[row1]
        a_copy(j).start()
        return c

    lax.fori_loop(1, GROUPS, serve, 0)
    row0, row1 = row_step(me)
    ra[2 * me] = enc[row0]
    ra[2 * me + 1] = enc[row1]

    def own_step(k, c):
        v = ids[me, k]
        owner = v // ROWS
        rank = jnp.int32(0)
        for e in range(SLOTS):
            same = (ids[me, e] // ROWS == owner) & (e < k)
            rank = rank + same.astype(jnp.int32)
        own_tab[0, k] = owner * 2 + rank
        return c

    lax.fori_loop(0, SLOTS, own_step, 0)

    def slot_step(q, c):
        slot = jnp.int32(0)
        for k in range(SLOTS):
            slot = jnp.where(own_tab[0, k] == q, k, slot)
        slot_tab[0, q] = slot
        return c

    lax.fori_loop(0, 2 * GROUPS, slot_step, 0)

    def shift(k, buf, landing):
        return remote(buf.at[pl.ds(192, 64)], landing, q_ss.at[k], q_rs.at[k], dev_prev)

    l_cot.wait()
    cs[...] = pltpu.roll(cot[...].astype(F32), TOK - (STRETCH - 1), 0).astype(BF16)
    shift(0, cs, cn).start()
    l_hid.wait()

    def query_step(i):
        l_wq[i].wait()
        part = dot(hid[:, i * QK:(i + 1) * QK], wq[pl.ds(i * QK, QK), :])
        if i == 0:
            qacc[...] = part
        else:
            qacc[...] += part

    def query_end():
        turned = pltpu.roll(qacc[...].astype(BF16).astype(F32), TOK - (STRETCH - 1), 0)
        qs[...] = turned.astype(BF16)
        shift(1, qs, qn).start()

    def build_selection():
        lane_k = lax.broadcasted_iota(jnp.int32, (8, 512), 1) // PIECE

        def col_step(q, cols):
            cnt = row_tab[2, q]
            first = jnp.where(cnt > 0, row_tab[0, q], -1)
            second = jnp.where(cnt > 1, row_tab[1, q], -1)
            cols = jnp.where(lane_k == 2 * q, first, cols)
            return jnp.where(lane_k == 2 * q + 1, second, cols)

        cols = lax.fori_loop(0, GROUPS, col_step, jnp.full((8, 512), -1, jnp.int32))
        row_i = lax.broadcasted_iota(jnp.int32, (TOK, 512), 0)
        col_i = lax.broadcasted_iota(jnp.int32, (TOK, 512), 1)
        match = (row_i // PIECE == cols[0:1, :]) & (row_i % PIECE == col_i % PIECE)
        onehot[...] = jnp.where(match, 1.0, 0.0).astype(BF16)

    def derive(c, carry):
        cols = pl.ds(pl.multiple_of(c * 256, 256), 256)
        pre = gd[:, cols]
        sq = pre * pre
        th = jnp.tanh(GELU_A * (pre + GELU_B * (sq * pre)))
        slope = pre * (0.5 * GELU_A) * (1.0 - th * th) * (1.0 + 3.0 * GELU_B * sq)
        gd[:, cols] = 0.5 * (1.0 + th) + slope
        return carry

    lax.fori_loop(0, FFN // 256, derive, 0)
    for i in range(QSTEPS):
        query_step(i)
    query_end()
    l_wk.wait()
    l_wv.wait()
    for lo in range(0, WIDTH, 128):
        w2t[:, lo:lo + 128] = w2[lo:lo + 128, :].T
    build_selection()
    each(ids_copy, wait_send)

    bo = t
    bp = y * 2 + 1 - xh

    parts = {"b": (0, HALF), "b0": (0, QUARTER), "b1": (QUARTER, QUARTER)}
    parts.update({"a0": (HALF, QUARTER), "a1": (HALF + QUARTER, QUARTER)})
    b_down, b_up, b_far = down * 2 + xh, up * 2 + xh, far * 2 + xh
    o_down, o_up, o_far = down * 2 + 1 - xh, up * 2 + 1 - xh, far * 2 + 1 - xh
    moves = {
        "oub": (bo, "b", dev_up), "odb": (bo, "b", dev_down),
        "xa0": (bo, "a0", dev_x), "xa1": (bo, "a1", dev_x), "xob": (bo, "b", dev_x),
        "oua0": (bo, "a0", dev_up), "oda1": (bo, "a1", dev_down),
        "oua1": (bo, "a1", dev_up), "oda0": (bo, "a0", dev_down),
        "rbu": (b_down, "b0", dev_up), "rbd": (b_up, "b1", dev_down),
        "xdb": (b_down, "b", dev_x), "xub": (b_up, "b", dev_x),
        "pu0": (bp, "a0", dev_up), "pd1": (bp, "a1", dev_down),
        "pu1": (bp, "a1", dev_up), "pd0": (bp, "a0", dev_down),
        "rau": (b_down, "a0", dev_up), "rad": (b_up, "a1", dev_down),
        "xf0": (b_far, "b0", dev_x), "xf1": (b_far, "b1", dev_x),
        "rpu": (o_down, "a0", dev_up), "rpd": (o_up, "a1", dev_down),
    }
    order = list(moves)

    def b_copy(k):
        b, part, dev = moves[k]
        lo, n = parts[part]
        at = order.index(k)
        ref = g.at[b, pl.ds(lo, n)]
        return remote(ref, ref, b_ss.at[at], b_rs.at[at], dev)

    def b_start(names):
        for k in names.split():
            b_copy(k).start()

    def b_wait(names):
        for k in names.split():
            b_copy(k).wait_recv()

    def select(k, c):
        g[bo, pl.ds(pl.multiple_of(k * PIECE, PIECE), PIECE)] = ra[own_tab[0, k]]
        return c

    def project(part, *blocks):
        rows = [g[b, pl.ds(part * HALF, HALF)] for b in blocks]
        rows = rows[0] if len(rows) == 1 else jnp.concatenate(rows, axis=0)
        out = dot(rows, w2[...]).astype(BF16)
        for i, b in enumerate(blocks):
            for u in range(2):
                at = i * HALF + u * 32
                kv[2 * part + u, pl.ds(pl.multiple_of(b * 32, 32), 32), :] = out[at:at + 32]

    def project_whole(b):
        out = dot(g[b], w2[...]).astype(BF16)
        for u in range(4):
            kv[u, pl.ds(pl.multiple_of(b * 32, 32), 32), :] = out[u * 32:(u + 1) * 32]

    each(a_copy, wait_recv)
    lax.fori_loop(0, SLOTS, select, 0)
    b_start("oub odb xa0 xa1")
    b_start("xob oua0 oda1")
    b_start("oua1 oda0")
    project_whole(bo)
    b_wait("oub")
    b_start("rbu xdb")
    b_wait("odb")
    b_start("rbd xub")
    b_wait("xa0")
    b_start("pu0")
    b_wait("xa1")
    b_start("pd1 pu1 pd0")
    b_wait("oua0")
    b_start("rau")
    b_wait("oda1")
    b_start("rad")
    project(0, b_down, b_up)
    b_wait("xob")
    project_whole(bp)
    b_wait("rbu")
    b_start("xf0")
    b_wait("rbd")
    b_start("xf1")
    b_wait("pu0")
    b_start("rpu")
    b_wait("pd1")
    b_start("rpd")
    b_wait("oua1 oda0")
    project(1, b_down, b_up)
    project(0, b_far)
    b_wait("xdb")
    project(0, o_down)
    b_wait("xub")
    project(0, o_up)
    each(a_copy, wait_send)
    shift(0, cs, cn).wait()
    shift(1, qs, qn).wait()
    keep = lax.broadcasted_iota(jnp.int32, (STRETCH, FEAT), 0) == 0
    more = s < SEQ - 1
    for buf, landing in ((qs, qn), (cs, cn)):
        mine = buf[192:256, :].astype(F32)
        theirs = jnp.where(more, landing[...].astype(F32), 0.0)
        buf[192:256, :] = jnp.where(keep, mine, theirs).astype(BF16)
    b_wait("pu1 pd0")
    project(1, o_down, o_up)

    scale = HD ** (-0.5)
    left = lax.broadcasted_iota(jnp.int32, (STRETCH, 2 * HD), 1) < HD

    def pair_rows(v):
        zero = jnp.zeros_like(v)
        return jnp.concatenate([jnp.where(left, v, zero), jnp.where(left, zero, v)], axis=0)

    def attend(u):
        rows = slice(u * STRETCH, u * STRETCH + STRETCH)
        for hp in range(2):
            lanes = slice(hp * 256, hp * 256 + 256)
            vlanes = slice(FEAT + hp * 256, FEAT + hp * 256 + 256)
            qb = pair_rows(qs[rows, lanes])
            db_ = pair_rows(cs[rows, lanes])
            kk = kv[u, :, lanes]
            vv = kv[u, :, vlanes]
            sc = dot_nt(kk, qb) * scale
            w = jnp.exp(sc - jnp.max(sc, axis=0, keepdims=True))
            p = w * (1.0 / jnp.sum(w, axis=0, keepdims=True))
            rounded = p.astype(BF16)
            prob[2 * u + hp] = rounded
            dp = dot_nt(vv, db_)
            centre = jnp.sum(p * dp, axis=0, keepdims=True)
            ds = (p * (dp - centre)).astype(BF16)
            kg = (dot(ds, qb) * scale).astype(BF16)
            vg = dot(rounded, db_).astype(BF16)
            at = slice((u % 2) * 32, (u % 2) * 32 + 32)
            for b in range(8):
                kgv[u // 2, b % 2, b // 2, at, lanes] = kg[b * 32:(b + 1) * 32]
                kgv[u // 2, b % 2, b // 2, at, vlanes] = vg[b * 32:(b + 1) * 32]

    o_back = remote(obuf.at[pl.ds(192, 64)], on, q_ss.at[2], q_rs.at[2], dev_next)

    def term(part, col):
        out = dot(kgv[part, col].reshape(4 * HALF, 2 * FEAT), w2t[...])
        terms[part, col] = out.reshape(4, HALF, WIDTH)

    oc = 1 - xh
    q0, q1 = pl.ds(0, QUARTER), pl.ds(QUARTER, QUARTER)
    both_q = pl.ds(0, HALF)
    c_moves = {}
    for k, name in enumerate(("xbf", "xbu", "xbd", "xbo")):
        c_moves[name] = (xb_s, xb_r, (k, both_q), dev_x)
    for h, name in enumerate("po"):
        c_moves["fu" + name] = (fa_s, fa_r, (h, q0), dev_up)
        c_moves["fd" + name] = (fa_s, fa_r, (h, q1), dev_down)
        c_moves["nu" + name] = (na_s, na_r, (h, 0, q1), dev_up)
        c_moves["nd" + name] = (na_s, na_r, (h, 1, q0), dev_down)
        c_moves["mu" + name] = (na_s, na_r, (h, 0, q0), dev_up)
        c_moves["md" + name] = (na_s, na_r, (h, 1, q1), dev_down)
    c_moves["fub"] = (fb_s, fb_r, (q0,), dev_up)
    c_moves["fdb"] = (fb_s, fb_r, (q1,), dev_down)
    c_moves["nub"] = (nb_s, nb_r, (0, q1), dev_up)
    c_moves["ndb"] = (nb_s, nb_r, (1, q0), dev_down)
    c_moves["mub"] = (nb_s, nb_r, (0, q0), dev_up)
    c_moves["mdb"] = (nb_s, nb_r, (1, q1), dev_down)
    c_moves["xs0"] = (xa_s, xa_r, (q0,), dev_x)
    c_moves["xs1"] = (xa_s, xa_r, (q1,), dev_x)
    c_order = list(c_moves)

    def c_copy(k):
        src, dst, part, dev = c_moves[k]
        at = c_order.index(k)
        return remote(src.at[part], dst.at[part], c_ss.at[at], c_rs.at[at], dev)

    def c_start(*names):
        for k in names:
            c_copy(k).start()

    def c_wait(*names):
        for k in names:
            c_copy(k).wait_recv()

    lo_q, hi_q = slice(0, QUARTER), slice(QUARTER, HALF)

    def far_out(h, col):
        fa_s[h] = terms[1, col, far].astype(BF16)

    def near_out(h, col):
        na_s[h, 0, hi_q] = terms[1, col, up, hi_q].astype(BF16)
        na_s[h, 1, lo_q] = terms[1, col, down, lo_q].astype(BF16)

    def merge_up(h, col):
        na_s[h, 0, lo_q] = (terms[1, col, up, lo_q] + fa_r[h, lo_q].astype(F32)).astype(BF16)

    def merge_down(h, col):
        na_s[h, 1, hi_q] = (terms[1, col, down, hi_q] + fa_r[h, hi_q].astype(F32)).astype(BF16)

    b_wait("rau rad")
    project(1, b_far)
    b_wait("rpu rpd")
    project(1, o_far)
    attend(2)
    attend(3)
    term(1, oc)
    far_out(0, oc)
    c_start("fup", "fdp")
    near_out(0, oc)
    c_start("nup", "ndp")
    b_wait("xf0 xf1")
    project(0, o_far)
    attend(0)
    attend(1)
    term(0, oc)
    for k, at in enumerate((far, up, down, y)):
        xb_s[k] = terms[0, oc, at].astype(BF16)
    c_start("xbf", "xbu", "xbd", "xbo")
    term(1, xh)
    far_out(1, xh)
    c_start("fuo", "fdo")
    term(0, xh)
    c_wait("xbf")
    fb_s[...] = (terms[0, xh, far] + xb_r[0].astype(F32)).astype(BF16)
    c_start("fub", "fdb")
    c_wait("fup")
    merge_up(0, oc)
    c_start("mup")
    c_wait("fdp")
    merge_down(0, oc)
    c_start("mdp")
    near_out(1, xh)
    c_start("nuo", "ndo")
    c_wait("xbu")
    v_up = terms[0, xh, up] + xb_r[1].astype(F32)
    terms[0, xh, up] = v_up
    nb_s[0, hi_q] = v_up[hi_q].astype(BF16)
    c_start("nub")
    c_wait("xbd")
    v_down = terms[0, xh, down] + xb_r[2].astype(F32)
    terms[0, xh, down] = v_down
    nb_s[1, lo_q] = v_down[lo_q].astype(BF16)
    c_start("ndb")
    c_wait("fuo")
    merge_up(1, xh)
    c_start("muo")
    c_wait("fdo")
    merge_down(1, xh)
    c_start("mdo")
    c_wait("fub")
    nb_s[0, lo_q] = (terms[0, xh, up, lo_q] + fb_r[lo_q].astype(F32)).astype(BF16)
    c_start("mub")
    c_wait("fdb")
    nb_s[1, hi_q] = (terms[0, xh, down, hi_q] + fb_r[hi_q].astype(F32)).astype(BF16)
    c_start("mdb")
    c_wait("nup", "ndp", "mup", "mdp")
    s_p = terms[1, oc, y] + na_r[0, 0].astype(F32) + na_r[0, 1].astype(F32)
    xa_s[...] = s_p.astype(BF16)
    c_start("xs0", "xs1")
    c_wait("xbo", "nub", "ndb", "mub", "mdb")
    s_b = terms[0, xh, y] + xb_r[3].astype(F32) + nb_r[0].astype(F32) + nb_r[1].astype(F32)
    fin[0:SLOTS // 2] = s_b.astype(BF16).reshape(SLOTS // 2, PIECE, WIDTH)
    c_wait("nuo", "ndo", "muo", "mdo")
    s_o = terms[1, xh, y] + na_r[1, 0].astype(F32) + na_r[1, 1].astype(F32)
    c_wait("xs0", "xs1")
    s_o = s_o + xa_r[...].astype(F32)
    fin[SLOTS // 2:] = s_o.astype(BF16).reshape(SLOTS // 2, PIECE, WIDTH)

    def give(j, c):
        q = (me + j) % GROUPS
        sd[2 * q] = fin[slot_tab[0, 2 * q]]
        sd[2 * q + 1] = fin[slot_tab[0, 2 * q + 1]]
        d_copy(j).start()
        return c

    lax.fori_loop(1, GROUPS, give, 0)
    rd[2 * me] = fin[slot_tab[0, 2 * me]]
    rd[2 * me + 1] = fin[slot_tab[0, 2 * me + 1]]

    for u in (3, 0, 1, 2):
        rows = slice(u * STRETCH, u * STRETCH + STRETCH)
        for hp in range(2):
            o = dot_tn(prob[2 * u + hp], kv[u, :, FEAT + hp * 256:FEAT + hp * 256 + 256])
            o = jnp.where(left, o[:STRETCH], o[STRETCH:])
            obuf[rows, hp * 256:hp * 256 + 256] = o.astype(BF16)
        if u == 3:
            o_back.start()
    for lo in range(0, FFN, 128):
        winT[lo:lo + 128, :] = win[:, lo:lo + 128].T
        woutT[:, lo:lo + 128] = wout[lo:lo + 128, :].T

    o_back.wait()
    edge = jnp.where(s > 0, on[...].astype(F32), 0.0)
    tail = jnp.where(keep, obuf[192:256, :].astype(F32), edge)
    whole = jnp.concatenate([obuf[0:192, :].astype(F32), tail], axis=0)
    att_out[...] = pltpu.roll(whole, STRETCH - 1, 0).astype(BF16)

    for k in order:
        b_copy(k).wait_send()
    for k in c_order:
        c_copy(k).wait_send()

    each(d_copy, wait_recv)
    rg = dot(onehot[...], rd[...].reshape(2 * GROUPS * PIECE, WIDTH))
    rgrad[...] = rg
    normed[...] = rg.astype(BF16)
    for lo in range(0, FFN, 256):
        d_act = dot(normed[...], woutT[:, lo:lo + 256])
        active[:, lo:lo + 256] = (d_act * gd[:, lo:lo + 256]).astype(BF16)
    mean = jnp.zeros((TOK, 1), F32)
    for lo, n in ((0, 512), (512, 384)):
        part = dot(active[...], winT[:, lo:lo + n]) * gain_row[:, lo:lo + n]
        dnorm[:, lo:lo + n] = part
        rows = db[:, :, lo:lo + n].reshape(TOK, n).astype(F32)
        mean = mean + jnp.sum(part * rows, axis=-1, keepdims=True)
    inv = inv_s[:, 0:1]
    xv = db[...].reshape(TOK, WIDTH).astype(F32)
    cubed = inv * inv * inv * (mean * (1.0 / WIDTH))
    out = rgrad[...] + inv * dnorm[...] - xv * cubed
    grad_out[...] = out.astype(BF16).reshape(ROWS, PIECE, WIDTH)
    each(d_copy, wait_send)


def body(hidden, w_query, w_key, w_value, enc_gain, w_in, w_out, db_states, neighbours, d_attended):
    hbm = pl.BlockSpec(memory_space=pl.ANY)
    vmem = pl.BlockSpec(memory_space=pltpu.VMEM)
    smem = pl.BlockSpec(memory_space=pltpu.SMEM)
    dma = pltpu.SemaphoreType.DMA
    vm = pltpu.VMEM
    scratch = [
        pltpu.SMEM((GROUPS, 128), jnp.int32),
        pltpu.SMEM((3, GROUPS), jnp.int32),
        pltpu.SMEM((1, SLOTS), jnp.int32),
        pltpu.SMEM((1, 2 * GROUPS), jnp.int32),
        vm((ROWS, PIECE, WIDTH), BF16),
        vm((WIDTH, FFN), BF16),
        vm((FFN, WIDTH), BF16),
        vm((FFN, WIDTH), BF16),
        vm((WIDTH, FFN), BF16),
        vm((WIDTH, 2 * FEAT), BF16),
        vm((2 * FEAT, WIDTH), BF16),
        vm((TOK, DM), BF16),
        vm((DM, FEAT), BF16),
        vm((TOK, FEAT), BF16),
        vm((TOK, WIDTH), BF16),
        vm((TOK, FFN), BF16),
        vm((TOK, FFN), F32),
        vm((TOK, 128), F32),
        vm((TOK, 512), BF16),
        vm((TOK, FEAT), F32),
        vm((TOK, FEAT), BF16),
        vm((TOK, FEAT), BF16),
        vm((STRETCH, FEAT), BF16),
        vm((STRETCH, FEAT), BF16),
        vm((TOK, FEAT), BF16),
        vm((STRETCH, FEAT), BF16),
        vm((ROWS, PIECE, WIDTH), BF16),
        vm((2 * GROUPS, PIECE, WIDTH), BF16),
        vm((2 * GROUPS, PIECE, WIDTH), BF16),
        vm((8, BLOCK, WIDTH), BF16),
        vm((4, 256, 2 * FEAT), BF16),
        vm((8, 256, 2 * STRETCH), BF16),
        vm((2, 2, 4, HALF, 2 * FEAT), BF16),
        vm((2, 2, 4, HALF, WIDTH), F32),
        vm((4, HALF, WIDTH), BF16), vm((4, HALF, WIDTH), BF16),
        vm((2, HALF, WIDTH), BF16), vm((2, HALF, WIDTH), BF16),
        vm((2, 2, HALF, WIDTH), BF16), vm((2, 2, HALF, WIDTH), BF16),
        vm((HALF, WIDTH), BF16), vm((HALF, WIDTH), BF16),
        vm((2, HALF, WIDTH), BF16), vm((2, HALF, WIDTH), BF16),
        vm((HALF, WIDTH), BF16), vm((HALF, WIDTH), BF16),
        vm((SLOTS, PIECE, WIDTH), BF16),
        vm((2 * GROUPS, PIECE, WIDTH), BF16),
        vm((2 * GROUPS, PIECE, WIDTH), BF16),
        vm((TOK, WIDTH), F32),
        vm((TOK, WIDTH), F32),
        dma((16,)),
        dma((16,)), dma((16,)),
        dma((16,)), dma((16,)),
        dma((16,)), dma((16,)),
        dma((24,)), dma((24,)),
        dma((24,)), dma((24,)),
        dma((3,)), dma((3,)),
    ]
    return pl.pallas_call(
        kernel,
        name="neighbour_attention",
        out_shape=(
            pltpu.VMEM((TOK, FEAT), BF16),
            pltpu.VMEM((ROWS, PIECE, WIDTH), BF16),
        ),
        in_specs=[smem, hbm, hbm, hbm, hbm, hbm, vmem, hbm, hbm, hbm],
        out_specs=(vmem, vmem),
        scratch_shapes=scratch,
        compiler_params=pltpu.CompilerParams(
            collective_id=0, has_side_effects=True, vmem_limit_bytes=56 * 1024 * 1024
        ),
    )(
        neighbours.T, db_states, hidden, w_query, w_key, w_value,
        enc_gain, w_in, w_out, d_attended,
    )


def solution(mesh):
    in_specs = (
        P(("role", "seq"), None),
        P(None, "tp"),
        P(None, "tp"),
        P(None, "tp"),
        P(),
        P(),
        P(),
        P(("role", "seq"), "tp", None),
        P(("role", "seq"), None),
        P(("role", "seq"), "tp"),
    )
    out_specs = (P(("role", "seq"), "tp"), P(("role", "seq"), "tp", None))
    return jax.shard_map(body, mesh=mesh, in_specs=in_specs, out_specs=out_specs, check_vma=False)
```

```python
import jax
import jax.numpy as jnp
from jax import lax
from jax.experimental import pallas as pl
from jax.experimental.pallas import tpu as pltpu
from jax.sharding import PartitionSpec as P

HD = 128
STRETCH = 64
EPS = 1e-06
MESH = pl.DeviceIdType.MESH
BF16 = jnp.bfloat16
F32 = jnp.float32
GELU_A = 0.7978845608028654
GELU_B = 0.044715

GROUPS = 16
SEQ = 8
ROWS = 16
SLOTS = 8
PIECE = 16
WIDTH = 896
FFN = 1792
TOK = 256
DM = 8192
FEAT = 512
BLOCK = SLOTS * PIECE
HALF = BLOCK // 2
QUARTER = BLOCK // 4
QK = 1024
QSTEPS = DM // QK


def dot(a, b):
    return jnp.dot(a, b, preferred_element_type=F32)


def dot_nt(a, b):
    return lax.dot_general(a, b, (((1,), (1,)), ((), ())), preferred_element_type=F32)


def dot_tn(a, b):
    return lax.dot_general(a, b, (((0,), (0,)), ((), ())), preferred_element_type=F32)


def kernel(
    nb, db_hbm, hid_hbm, wq_hbm, wk_hbm, wv_hbm, gain, win_hbm, wout_hbm, cot_hbm,
    att_out, grad_out,
    ids, row_tab, own_tab, slot_tab,
    db, win, wout, winT, woutT, w2, w2t, hid, wq, cot,
    normed, active, gd, inv_s, onehot, qacc, qs, cs, qn, cn, obuf, on,
    enc, sa, ra, g, kv, prob, kgv, terms,
    xb_s, xb_r, fa_s, fa_r, na_s, na_r, fb_s, fb_r, nb_s, nb_r, xa_s, xa_r,
    fin, sd, rd, rgrad, dnorm,
    lsem, ids_ss, ids_rs, a_ss, a_rs, d_ss, d_rs, b_ss, b_rs, c_ss, c_rs, q_ss, q_rs,
):
    r = lax.axis_index("role")
    s = lax.axis_index("seq")
    t = lax.axis_index("tp")
    y = t // 2
    xh = t % 2
    me = r * SEQ + s
    up = (y + 1) % 4
    down = (y + 3) % 4
    far = (y + 2) % 4
    dev_up = (r, s, up * 2 + xh)
    dev_down = (r, s, down * 2 + xh)
    dev_x = (r, s, y * 2 + 1 - xh)
    dev_next = (r, (s + 1) % SEQ, t)
    dev_prev = (r, (s + SEQ - 1) % SEQ, t)

    def remote(src, dst, ss, rs, dev):
        return pltpu.make_async_remote_copy(
            src_ref=src, dst_ref=dst, send_sem=ss, recv_sem=rs, device_id=dev, device_id_type=MESH
        )

    loads = []

    def load(src, dst):
        cp = pltpu.make_async_copy(src, dst, lsem.at[len(loads)])
        cp.start()
        loads.append(cp)
        return cp

    l_db = load(db_hbm, db)
    l_win = load(win_hbm, win)

    barrier = pltpu.get_barrier_semaphore()

    def greet(dev):
        pl.semaphore_signal(barrier, inc=1, device_id=dev, device_id_type=MESH)

    def peer(j):
        q = (me + j) % GROUPS
        return q, (q // SEQ, q % SEQ, t)

    def greet_group(j, c):
        greet(peer(j)[1])
        return c

    lax.fori_loop(1, GROUPS, greet_group, 0)
    greet(dev_up)
    greet(dev_down)
    greet(dev_x)

    def copy_ids(i, c):
        ids[me, i] = nb[i % 2, i // 2]
        return c

    lax.fori_loop(0, SLOTS, copy_ids, 0)

    pl.semaphore_wait(barrier, 18)

    def each(make, act):
        def step(j, c):
            act(make(j))
            return c

        lax.fori_loop(1, GROUPS, step, 0)

    def ids_copy(j):
        return remote(ids.at[me], ids.at[me], ids_ss.at[j], ids_rs.at[j], peer(j)[1])

    start = lambda cp: cp.start()
    wait_recv = lambda cp: cp.wait_recv()
    wait_send = lambda cp: cp.wait_send()

    each(ids_copy, start)

    l_db.wait()
    xv = db[...].reshape(TOK, WIDTH).astype(F32)
    inverse = lax.rsqrt(jnp.mean(xv * xv, axis=-1, keepdims=True) + EPS)
    inv_s[...] = jnp.broadcast_to(inverse, (TOK, 128))
    gain_row = gain[...].reshape(1, WIDTH)
    normed[...] = (xv * inverse * gain_row).astype(BF16)
    l_win.wait()
    l_wout = load(wout_hbm, wout)

    for lo in range(0, FFN, 256):
        cols = slice(lo, lo + 256)
        pre = dot(normed[...], win[:, cols])
        gd[:, cols] = pre
        th = jnp.tanh(GELU_A * (pre + GELU_B * (pre * pre * pre)))
        active[:, cols] = (pre * (0.5 * (1.0 + th))).astype(BF16)
    l_wout.wait()

    l_cot = load(cot_hbm, cot)
    l_hid = load(hid_hbm, hid)
    l_wq = [
        load(wq_hbm.at[pl.ds(i * QK, QK)], wq.at[pl.ds(i * QK, QK)]) for i in range(QSTEPS)
    ]
    l_wk = load(wk_hbm, w2.at[:, pl.ds(0, FEAT)])
    l_wv = load(wv_hbm, w2.at[:, pl.ds(FEAT, FEAT)])

    rows = db[...].reshape(TOK, WIDTH).astype(F32)
    coded = rows + dot(active[...], wout[...])
    enc[...] = coded.astype(BF16).reshape(ROWS, PIECE, WIDTH)

    def row_step(q):
        cnt = jnp.int32(0)
        row0 = jnp.int32(0)
        row1 = jnp.int32(0)
        for k in range(SLOTS):
            v = ids[q, k] - me * ROWS
            hit = (v >= 0) & (v < ROWS)
            row0 = jnp.where(hit & (cnt == 0), v, row0)
            row1 = jnp.where(hit & (cnt == 1), v, row1)
            cnt = cnt + hit.astype(jnp.int32)
        row_tab[0, q] = row0
        row_tab[1, q] = row1
        row_tab[2, q] = cnt
        return row0, row1

    def exchange(src, dst, ss, rs):
        def make(j):
            q, dev = peer(j)
            return remote(src.at[pl.ds(2 * q, 2)], dst.at[pl.ds(2 * me, 2)], ss.at[j], rs.at[j], dev)

        return make

    a_copy = exchange(sa, ra, a_ss, a_rs)
    d_copy = exchange(sd, rd, d_ss, d_rs)

    def serve(j, c):
        ids_copy(GROUPS - j).wait_recv()
        q = (me + j) % GROUPS
        row0, row1 = row_step(q)
        sa[2 * q] = enc[row0]
        sa[2 * q + 1] = enc[row1]
        a_copy(j).start()
        return c

    lax.fori_loop(1, GROUPS, serve, 0)
    row0, row1 = row_step(me)
    ra[2 * me] = enc[row0]
    ra[2 * me + 1] = enc[row1]

    def own_step(k, c):
        v = ids[me, k]
        owner = v // ROWS
        rank = jnp.int32(0)
        for e in range(SLOTS):
            same = (ids[me, e] // ROWS == owner) & (e < k)
            rank = rank + same.astype(jnp.int32)
        own_tab[0, k] = owner * 2 + rank
        return c

    lax.fori_loop(0, SLOTS, own_step, 0)

    def slot_step(q, c):
        slot = jnp.int32(0)
        for k in range(SLOTS):
            slot = jnp.where(own_tab[0, k] == q, k, slot)
        slot_tab[0, q] = slot
        return c

    lax.fori_loop(0, 2 * GROUPS, slot_step, 0)

    def shift(k, buf, landing):
        return remote(buf.at[pl.ds(192, 64)], landing, q_ss.at[k], q_rs.at[k], dev_prev)

    l_cot.wait()
    cs[...] = pltpu.roll(cot[...].astype(F32), TOK - (STRETCH - 1), 0).astype(BF16)
    shift(0, cs, cn).start()
    l_hid.wait()

    def query_step(i):
        l_wq[i].wait()
        part = dot(hid[:, i * QK:(i + 1) * QK], wq[pl.ds(i * QK, QK), :])
        if i == 0:
            qacc[...] = part
        else:
            qacc[...] += part

    def query_end():
        turned = pltpu.roll(qacc[...].astype(BF16).astype(F32), TOK - (STRETCH - 1), 0)
        qs[...] = turned.astype(BF16)
        shift(1, qs, qn).start()

    def build_selection():
        lane_k = lax.broadcasted_iota(jnp.int32, (8, 512), 1) // PIECE

        def col_step(q, cols):
            cnt = row_tab[2, q]
            first = jnp.where(cnt > 0, row_tab[0, q], -1)
            second = jnp.where(cnt > 1, row_tab[1, q], -1)
            cols = jnp.where(lane_k == 2 * q, first, cols)
            return jnp.where(lane_k == 2 * q + 1, second, cols)

        cols = lax.fori_loop(0, GROUPS, col_step, jnp.full((8, 512), -1, jnp.int32))
        row_i = lax.broadcasted_iota(jnp.int32, (TOK, 512), 0)
        col_i = lax.broadcasted_iota(jnp.int32, (TOK, 512), 1)
        match = (row_i // PIECE == cols[0:1, :]) & (row_i % PIECE == col_i % PIECE)
        onehot[...] = jnp.where(match, 1.0, 0.0).astype(BF16)

    def derive(c, carry):
        cols = pl.ds(pl.multiple_of(c * 256, 256), 256)
        pre = gd[:, cols]
        sq = pre * pre
        th = jnp.tanh(GELU_A * (pre + GELU_B * (sq * pre)))
        slope = pre * (0.5 * GELU_A) * (1.0 - th * th) * (1.0 + 3.0 * GELU_B * sq)
        gd[:, cols] = 0.5 * (1.0 + th) + slope
        return carry

    lax.fori_loop(0, FFN // 256, derive, 0)
    for i in range(QSTEPS):
        query_step(i)
    query_end()
    l_wk.wait()
    l_wv.wait()
    for lo in range(0, WIDTH, 128):
        w2t[:, lo:lo + 128] = w2[lo:lo + 128, :].T
    build_selection()
    each(ids_copy, wait_send)

    bo = t
    bp = y * 2 + 1 - xh

    parts = {"b": (0, HALF), "b0": (0, QUARTER), "b1": (QUARTER, QUARTER)}
    parts.update({"a0": (HALF, QUARTER), "a1": (HALF + QUARTER, QUARTER)})
    b_down, b_up, b_far = down * 2 + xh, up * 2 + xh, far * 2 + xh
    o_down, o_up, o_far = down * 2 + 1 - xh, up * 2 + 1 - xh, far * 2 + 1 - xh
    moves = {
        "oub": (bo, "b", dev_up), "odb": (bo, "b", dev_down),
        "xa0": (bo, "a0", dev_x), "xa1": (bo, "a1", dev_x), "xob": (bo, "b", dev_x),
        "oua0": (bo, "a0", dev_up), "oda1": (bo, "a1", dev_down),
        "oua1": (bo, "a1", dev_up), "oda0": (bo, "a0", dev_down),
        "rbu": (b_down, "b0", dev_up), "rbd": (b_up, "b1", dev_down),
        "xdb": (b_down, "b", dev_x), "xub": (b_up, "b", dev_x),
        "pu0": (bp, "a0", dev_up), "pd1": (bp, "a1", dev_down),
        "pu1": (bp, "a1", dev_up), "pd0": (bp, "a0", dev_down),
        "rau": (b_down, "a0", dev_up), "rad": (b_up, "a1", dev_down),
        "xf0": (b_far, "b0", dev_x), "xf1": (b_far, "b1", dev_x),
        "rpu": (o_down, "a0", dev_up), "rpd": (o_up, "a1", dev_down),
    }
    order = list(moves)

    def b_copy(k):
        b, part, dev = moves[k]
        lo, n = parts[part]
        at = order.index(k)
        ref = g.at[b, pl.ds(lo, n)]
        return remote(ref, ref, b_ss.at[at], b_rs.at[at], dev)

    def b_start(names):
        for k in names.split():
            b_copy(k).start()

    def b_wait(names):
        for k in names.split():
            b_copy(k).wait_recv()

    def select(k, c):
        g[bo, pl.ds(pl.multiple_of(k * PIECE, PIECE), PIECE)] = ra[own_tab[0, k]]
        return c

    def project(part, *blocks):
        rows = [g[b, pl.ds(part * HALF, HALF)] for b in blocks]
        rows = rows[0] if len(rows) == 1 else jnp.concatenate(rows, axis=0)
        out = dot(rows, w2[...]).astype(BF16)
        for i, b in enumerate(blocks):
            for u in range(2):
                at = i * HALF + u * 32
                kv[2 * part + u, pl.ds(pl.multiple_of(b * 32, 32), 32), :] = out[at:at + 32]

    def project_whole(b):
        out = dot(g[b], w2[...]).astype(BF16)
        for u in range(4):
            kv[u, pl.ds(pl.multiple_of(b * 32, 32), 32), :] = out[u * 32:(u + 1) * 32]

    each(a_copy, wait_recv)
    lax.fori_loop(0, SLOTS, select, 0)
    b_start("oub odb xa0 xa1")
    b_start("xob oua0 oda1")
    b_start("oua1 oda0")
    project_whole(bo)
    b_wait("oub")
    b_start("rbu xdb")
    b_wait("odb")
    b_start("rbd xub")
    b_wait("xa0")
    b_start("pu0")
    b_wait("xa1")
    b_start("pd1 pu1 pd0")
    b_wait("oua0")
    b_start("rau")
    b_wait("oda1")
    b_start("rad")
    project(0, b_down, b_up)
    b_wait("xob")
    project_whole(bp)
    b_wait("rbu")
    b_start("xf0")
    b_wait("rbd")
    b_start("xf1")
    b_wait("pu0")
    b_start("rpu")
    b_wait("pd1")
    b_start("rpd")
    b_wait("oua1 oda0")
    project(1, b_down, b_up)
    project(0, b_far)
    b_wait("xdb")
    project(0, o_down)
    b_wait("xub")
    project(0, o_up)
    shift(0, cs, cn).wait()
    shift(1, qs, qn).wait()
    keep = lax.broadcasted_iota(jnp.int32, (STRETCH, FEAT), 0) == 0
    more = s < SEQ - 1
    for buf, landing in ((qs, qn), (cs, cn)):
        mine = buf[192:256, :].astype(F32)
        theirs = jnp.where(more, landing[...].astype(F32), 0.0)
        buf[192:256, :] = jnp.where(keep, mine, theirs).astype(BF16)
    b_wait("pu1 pd0")
    project(1, o_down, o_up)

    scale = HD ** (-0.5)
    left = lax.broadcasted_iota(jnp.int32, (STRETCH, 2 * HD), 1) < HD

    def pair_rows(v):
        zero = jnp.zeros_like(v)
        return jnp.concatenate([jnp.where(left, v, zero), jnp.where(left, zero, v)], axis=0)

    def attend(u):
        rows = slice(u * STRETCH, u * STRETCH + STRETCH)
        for hp in range(2):
            lanes = slice(hp * 256, hp * 256 + 256)
            vlanes = slice(FEAT + hp * 256, FEAT + hp * 256 + 256)
            qb = pair_rows(qs[rows, lanes])
            db_ = pair_rows(cs[rows, lanes])
            kk = kv[u, :, lanes]
            vv = kv[u, :, vlanes]
            sc = dot_nt(kk, qb) * scale
            w = jnp.exp(sc - jnp.max(sc, axis=0, keepdims=True))
            p = w * (1.0 / jnp.sum(w, axis=0, keepdims=True))
            rounded = p.astype(BF16)
            prob[2 * u + hp] = rounded
            dp = dot_nt(vv, db_)
            centre = jnp.sum(p * dp, axis=0, keepdims=True)
            ds = (p * (dp - centre)).astype(BF16)
            kg = (dot(ds, qb) * scale).astype(BF16)
            vg = dot(rounded, db_).astype(BF16)
            at = slice((u % 2) * 32, (u % 2) * 32 + 32)
            for b in range(8):
                kgv[u // 2, b % 2, b // 2, at, lanes] = kg[b * 32:(b + 1) * 32]
                kgv[u // 2, b % 2, b // 2, at, vlanes] = vg[b * 32:(b + 1) * 32]

    o_back = remote(obuf.at[pl.ds(192, 64)], on, q_ss.at[2], q_rs.at[2], dev_next)

    def term(part, col):
        out = dot(kgv[part, col].reshape(4 * HALF, 2 * FEAT), w2t[...])
        terms[part, col] = out.reshape(4, HALF, WIDTH)

    oc = 1 - xh
    q0, q1 = pl.ds(0, QUARTER), pl.ds(QUARTER, QUARTER)
    both_q = pl.ds(0, HALF)
    c_moves = {}
    for k, name in enumerate(("xbf", "xbu", "xbd", "xbo")):
        c_moves[name] = (xb_s, xb_r, (k, both_q), dev_x)
    for h, name in enumerate("po"):
        c_moves["fu" + name] = (fa_s, fa_r, (h, q0), dev_up)
        c_moves["fd" + name] = (fa_s, fa_r, (h, q1), dev_down)
        c_moves["nu" + name] = (na_s, na_r, (h, 0, q1), dev_up)
        c_moves["nd" + name] = (na_s, na_r, (h, 1, q0), dev_down)
        c_moves["mu" + name] = (na_s, na_r, (h, 0, q0), dev_up)
        c_moves["md" + name] = (na_s, na_r, (h, 1, q1), dev_down)
    c_moves["fub"] = (fb_s, fb_r, (q0,), dev_up)
    c_moves["fdb"] = (fb_s, fb_r, (q1,), dev_down)
    c_moves["nub"] = (nb_s, nb_r, (0, q1), dev_up)
    c_moves["ndb"] = (nb_s, nb_r, (1, q0), dev_down)
    c_moves["mub"] = (nb_s, nb_r, (0, q0), dev_up)
    c_moves["mdb"] = (nb_s, nb_r, (1, q1), dev_down)
    c_moves["xs0"] = (xa_s, xa_r, (q0,), dev_x)
    c_moves["xs1"] = (xa_s, xa_r, (q1,), dev_x)
    c_order = list(c_moves)

    def c_copy(k):
        src, dst, part, dev = c_moves[k]
        at = c_order.index(k)
        return remote(src.at[part], dst.at[part], c_ss.at[at], c_rs.at[at], dev)

    def c_start(*names):
        for k in names:
            c_copy(k).start()

    def c_wait(*names):
        for k in names:
            c_copy(k).wait_recv()

    lo_q, hi_q = slice(0, QUARTER), slice(QUARTER, HALF)

    def far_out(h, col):
        fa_s[h] = terms[1, col, far].astype(BF16)

    def near_out(h, col):
        na_s[h, 0, hi_q] = terms[1, col, up, hi_q].astype(BF16)
        na_s[h, 1, lo_q] = terms[1, col, down, lo_q].astype(BF16)

    def merge_up(h, col):
        na_s[h, 0, lo_q] = (terms[1, col, up, lo_q] + fa_r[h, lo_q].astype(F32)).astype(BF16)

    def merge_down(h, col):
        na_s[h, 1, hi_q] = (terms[1, col, down, hi_q] + fa_r[h, hi_q].astype(F32)).astype(BF16)

    b_wait("rau rad")
    project(1, b_far)
    b_wait("rpu rpd")
    project(1, o_far)
    attend(2)
    attend(3)
    term(1, oc)
    far_out(0, oc)
    c_start("fup", "fdp")
    near_out(0, oc)
    c_start("nup", "ndp")
    b_wait("xf0 xf1")
    project(0, o_far)
    attend(0)
    attend(1)
    term(0, oc)
    for k, at in enumerate((far, up, down, y)):
        xb_s[k] = terms[0, oc, at].astype(BF16)
    c_start("xbf", "xbu", "xbd", "xbo")
    term(1, xh)
    far_out(1, xh)
    c_start("fuo", "fdo")
    term(0, xh)
    c_wait("xbf")
    fb_s[...] = (terms[0, xh, far] + xb_r[0].astype(F32)).astype(BF16)
    c_start("fub", "fdb")
    c_wait("fup")
    merge_up(0, oc)
    c_start("mup")
    c_wait("fdp")
    merge_down(0, oc)
    c_start("mdp")
    near_out(1, xh)
    c_start("nuo", "ndo")
    c_wait("xbu")
    v_up = terms[0, xh, up] + xb_r[1].astype(F32)
    terms[0, xh, up] = v_up
    nb_s[0, hi_q] = v_up[hi_q].astype(BF16)
    c_start("nub")
    c_wait("xbd")
    v_down = terms[0, xh, down] + xb_r[2].astype(F32)
    terms[0, xh, down] = v_down
    nb_s[1, lo_q] = v_down[lo_q].astype(BF16)
    c_start("ndb")
    c_wait("fuo")
    merge_up(1, xh)
    c_start("muo")
    c_wait("fdo")
    merge_down(1, xh)
    c_start("mdo")
    c_wait("fub")
    nb_s[0, lo_q] = (terms[0, xh, up, lo_q] + fb_r[lo_q].astype(F32)).astype(BF16)
    c_start("mub")
    c_wait("fdb")
    nb_s[1, hi_q] = (terms[0, xh, down, hi_q] + fb_r[hi_q].astype(F32)).astype(BF16)
    c_start("mdb")
    c_wait("nup", "ndp", "mup", "mdp")
    s_p = terms[1, oc, y] + na_r[0, 0].astype(F32) + na_r[0, 1].astype(F32)
    xa_s[...] = s_p.astype(BF16)
    c_start("xs0", "xs1")
    c_wait("xbo", "nub", "ndb", "mub", "mdb")
    s_b = terms[0, xh, y] + xb_r[3].astype(F32) + nb_r[0].astype(F32) + nb_r[1].astype(F32)
    fin[0:SLOTS // 2] = s_b.astype(BF16).reshape(SLOTS // 2, PIECE, WIDTH)
    c_wait("nuo", "ndo", "muo", "mdo")
    s_o = terms[1, xh, y] + na_r[1, 0].astype(F32) + na_r[1, 1].astype(F32)
    c_wait("xs0", "xs1")
    s_o = s_o + xa_r[...].astype(F32)
    fin[SLOTS // 2:] = s_o.astype(BF16).reshape(SLOTS // 2, PIECE, WIDTH)

    def give(j, c):
        q = (me + j) % GROUPS
        sd[2 * q] = fin[slot_tab[0, 2 * q]]
        sd[2 * q + 1] = fin[slot_tab[0, 2 * q + 1]]
        d_copy(j).start()
        return c

    lax.fori_loop(1, GROUPS, give, 0)
    rd[2 * me] = fin[slot_tab[0, 2 * me]]
    rd[2 * me + 1] = fin[slot_tab[0, 2 * me + 1]]

    for u in (3, 0, 1, 2):
        rows = slice(u * STRETCH, u * STRETCH + STRETCH)
        for hp in range(2):
            o = dot_tn(prob[2 * u + hp], kv[u, :, FEAT + hp * 256:FEAT + hp * 256 + 256])
            o = jnp.where(left, o[:STRETCH], o[STRETCH:])
            obuf[rows, hp * 256:hp * 256 + 256] = o.astype(BF16)
        if u == 3:
            o_back.start()
    for lo in range(0, FFN, 128):
        winT[lo:lo + 128, :] = win[:, lo:lo + 128].T
        woutT[:, lo:lo + 128] = wout[lo:lo + 128, :].T

    o_back.wait()
    edge = jnp.where(s > 0, on[...].astype(F32), 0.0)
    tail = jnp.where(keep, obuf[192:256, :].astype(F32), edge)
    whole = jnp.concatenate([obuf[0:192, :].astype(F32), tail], axis=0)
    att_out[...] = pltpu.roll(whole, STRETCH - 1, 0).astype(BF16)

    each(a_copy, wait_send)
    for k in order:
        b_copy(k).wait_send()
    for k in c_order:
        c_copy(k).wait_send()

    each(d_copy, wait_recv)
    rg = dot(onehot[...], rd[...].reshape(2 * GROUPS * PIECE, WIDTH))
    rgrad[...] = rg
    normed[...] = rg.astype(BF16)
    for lo in range(0, FFN, 256):
        d_act = dot(normed[...], woutT[:, lo:lo + 256])
        active[:, lo:lo + 256] = (d_act * gd[:, lo:lo + 256]).astype(BF16)
    mean = jnp.zeros((TOK, 1), F32)
    for lo, n in ((0, 512), (512, 384)):
        part = dot(active[...], winT[:, lo:lo + n]) * gain_row[:, lo:lo + n]
        dnorm[:, lo:lo + n] = part
        rows = db[:, :, lo:lo + n].reshape(TOK, n).astype(F32)
        mean = mean + jnp.sum(part * rows, axis=-1, keepdims=True)
    inv = inv_s[:, 0:1]
    xv = db[...].reshape(TOK, WIDTH).astype(F32)
    cubed = inv * inv * inv * (mean * (1.0 / WIDTH))
    out = rgrad[...] + inv * dnorm[...] - xv * cubed
    grad_out[...] = out.astype(BF16).reshape(ROWS, PIECE, WIDTH)
    each(d_copy, wait_send)


def body(hidden, w_query, w_key, w_value, enc_gain, w_in, w_out, db_states, neighbours, d_attended):
    hbm = pl.BlockSpec(memory_space=pl.ANY)
    vmem = pl.BlockSpec(memory_space=pltpu.VMEM)
    smem = pl.BlockSpec(memory_space=pltpu.SMEM)
    dma = pltpu.SemaphoreType.DMA
    vm = pltpu.VMEM
    scratch = [
        pltpu.SMEM((GROUPS, 128), jnp.int32),
        pltpu.SMEM((3, GROUPS), jnp.int32),
        pltpu.SMEM((1, SLOTS), jnp.int32),
        pltpu.SMEM((1, 2 * GROUPS), jnp.int32),
        vm((ROWS, PIECE, WIDTH), BF16),
        vm((WIDTH, FFN), BF16),
        vm((FFN, WIDTH), BF16),
        vm((FFN, WIDTH), BF16),
        vm((WIDTH, FFN), BF16),
        vm((WIDTH, 2 * FEAT), BF16),
        vm((2 * FEAT, WIDTH), BF16),
        vm((TOK, DM), BF16),
        vm((DM, FEAT), BF16),
        vm((TOK, FEAT), BF16),
        vm((TOK, WIDTH), BF16),
        vm((TOK, FFN), BF16),
        vm((TOK, FFN), F32),
        vm((TOK, 128), F32),
        vm((TOK, 512), BF16),
        vm((TOK, FEAT), F32),
        vm((TOK, FEAT), BF16),
        vm((TOK, FEAT), BF16),
        vm((STRETCH, FEAT), BF16),
        vm((STRETCH, FEAT), BF16),
        vm((TOK, FEAT), BF16),
        vm((STRETCH, FEAT), BF16),
        vm((ROWS, PIECE, WIDTH), BF16),
        vm((2 * GROUPS, PIECE, WIDTH), BF16),
        vm((2 * GROUPS, PIECE, WIDTH), BF16),
        vm((8, BLOCK, WIDTH), BF16),
        vm((4, 256, 2 * FEAT), BF16),
        vm((8, 256, 2 * STRETCH), BF16),
        vm((2, 2, 4, HALF, 2 * FEAT), BF16),
        vm((2, 2, 4, HALF, WIDTH), F32),
        vm((4, HALF, WIDTH), BF16), vm((4, HALF, WIDTH), BF16),
        vm((2, HALF, WIDTH), BF16), vm((2, HALF, WIDTH), BF16),
        vm((2, 2, HALF, WIDTH), BF16), vm((2, 2, HALF, WIDTH), BF16),
        vm((HALF, WIDTH), BF16), vm((HALF, WIDTH), BF16),
        vm((2, HALF, WIDTH), BF16), vm((2, HALF, WIDTH), BF16),
        vm((HALF, WIDTH), BF16), vm((HALF, WIDTH), BF16),
        vm((SLOTS, PIECE, WIDTH), BF16),
        vm((2 * GROUPS, PIECE, WIDTH), BF16),
        vm((2 * GROUPS, PIECE, WIDTH), BF16),
        vm((TOK, WIDTH), F32),
        vm((TOK, WIDTH), F32),
        dma((16,)),
        dma((16,)), dma((16,)),
        dma((16,)), dma((16,)),
        dma((16,)), dma((16,)),
        dma((24,)), dma((24,)),
        dma((24,)), dma((24,)),
        dma((3,)), dma((3,)),
    ]
    return pl.pallas_call(
        kernel,
        name="neighbour_attention",
        out_shape=(
            pltpu.VMEM((TOK, FEAT), BF16),
            pltpu.VMEM((ROWS, PIECE, WIDTH), BF16),
        ),
        in_specs=[smem, hbm, hbm, hbm, hbm, hbm, vmem, hbm, hbm, hbm],
        out_specs=(vmem, vmem),
        scratch_shapes=scratch,
        compiler_params=pltpu.CompilerParams(
            collective_id=0, has_side_effects=True, vmem_limit_bytes=56 * 1024 * 1024
        ),
    )(
        neighbours.T, db_states, hidden, w_query, w_key, w_value,
        enc_gain, w_in, w_out, d_attended,
    )


def solution(mesh):
    in_specs = (
        P(("role", "seq"), None),
        P(None, "tp"),
        P(None, "tp"),
        P(None, "tp"),
        P(),
        P(),
        P(),
        P(("role", "seq"), "tp", None),
        P(("role", "seq"), None),
        P(("role", "seq"), "tp"),
    )
    out_specs = (P(("role", "seq"), "tp"), P(("role", "seq"), "tp", None))
    return jax.shard_map(body, mesh=mesh, in_specs=in_specs, out_specs=out_specs, check_vma=False)
```
